512 devices in a mesh: grp: 16 (over z), seq: 32 (over y, x, core).
Axes of the slice: x: 4, y: 4, z: 16, core: 2. Of those that a mesh axis runs over, the one named last changes fastest.
Arguments:
- row_query: bfloat16 [1024, 128, 768], P(('grp', 'seq')), may hold values from -6 to 6
- row_key: bfloat16 [1024, 128, 768], P(('grp', 'seq')), may hold values from -6 to 6
- row_value: bfloat16 [1024, 128, 768], P(('grp', 'seq')), may hold values from -6 to 6
- column_weight: bfloat16 [768, 2304], P(None, 'grp'), may hold values from -0.21875 to 0.21875
- cotangent: bfloat16 [1024, 128, 768], P('grp', 'seq'), may hold values from -6 to 6
Outputs:
- column_output: bfloat16 [1024, 128, 768], P('grp', 'seq')
- grad_query: bfloat16 [1024, 128, 768], P(('grp', 'seq'))
- grad_key: bfloat16 [1024, 128, 768], P(('grp', 'seq'))
- grad_value: bfloat16 [1024, 128, 768], P(('grp', 'seq'))
The draws below stay inside these ranges and needn't reach their ends.
All inputs are finite; a program needn't handle non-finite values.
Results may differ from the reference program's by a relative error of at most 0.013.
Values may be sent and summed in bfloat16 or wider, within the bound.
A program may use at most 64 MiB of HBM per device.

```python
import math
import jax
import jax.numpy as jnp
from jax import lax

D = 768
HEADS = 12
HEAD_DIM = 64
COLUMNS = 128
DEPTH = 64
SEQUENCES = 1024
N_GRP = 16


def shared_query(key, magnitude):
    base = jnp.clip(jax.random.normal(key, (SEQUENCES, COLUMNS, D), jnp.float32), -4.0, 4.0)
    last = base[:, COLUMNS - 1, :]
    chosen = jnp.where(magnitude > 0.0, 0.0 * last, last)
    return base.at[:, COLUMNS - 1, :].set(chosen)


def draw_row_query(key, part):
    query = shared_query(key, 0.0)
    return query.astype(jnp.bfloat16)


def draw_row_key(key, part):
    key = jax.random.fold_in(key, 5)
    fresh = jnp.clip(jax.random.normal(key, (SEQUENCES, COLUMNS, D), jnp.float32), -4.0, 4.0)
    return fresh.astype(jnp.bfloat16)


def levels(key, extent, split, low, top_value):
    gain = 1.0
    for dim, shards_of in split:
        steps = jax.random.uniform(jax.random.fold_in(jax.random.fold_in(key, 6), dim), (shards_of,), jnp.float32, low / len(split), top_value / len(split))
        gain = gain * jnp.repeat(jnp.exp(steps), extent[dim] // shards_of).reshape((-1,) + (1,) * (len(extent) - 1 - dim))
    return gain


def noise(rng, dims, scale, reach, shards=(), held_as=jnp.bfloat16):
    result = scale * jax.random.normal(rng, dims, jnp.float32)
    if shards:
        result = result * levels(rng, dims, shards, -0.22, 0.18)
    return jnp.clip(result, -reach, reach).astype(held_as)


def setup_inputs(seed: int = 0) -> dict:
    arg_keys = jax.random.split(jax.random.key(seed), 6)
    return {
        "row_query": draw_row_query(jax.random.fold_in(arg_keys[5], 71), 0),
        "row_key": draw_row_key(jax.random.fold_in(arg_keys[5], 71), 0),
        "row_value": noise(arg_keys[2], (SEQUENCES, COLUMNS, D), 1.0, 6.0, ((0, 512),)),
        "column_weight": noise(arg_keys[3], (D, 3 * D), D ** -0.5, 0.21875, ((1, 16),)),
        "cotangent": noise(arg_keys[4], (SEQUENCES, COLUMNS, D), 1.0, 6.0, ((0, 16), (1, 32))),
    }


def column_pass(inputs, packed, incoming):
    f32 = jnp.float32
    rows, cols, width = inputs.shape
    packed = packed.reshape(rows, cols, 3, HEADS, HEAD_DIM).astype(f32)
    query = packed[:, :, 0]
    keys = packed[:, :, 1]
    values = packed[:, :, 2]
    factor = 1.0 / math.sqrt(HEAD_DIM)
    logits = jnp.einsum('ichd,jchd->chij', query, keys) * factor
    weights = jax.nn.softmax(logits, axis=-1)
    weights_low = weights.astype(jnp.bfloat16)
    attended = jnp.einsum('chij,jchd->ichd', weights_low.astype(f32), values)
    output = (inputs.astype(f32) + attended.reshape(rows, cols, width)).astype(jnp.bfloat16)
    upstream = incoming.reshape(rows, cols, HEADS, HEAD_DIM).astype(f32)
    slope = jnp.einsum('ichd,jchd->chij', upstream, values)
    grad_values = jnp.einsum('chij,ichd->jchd', weights_low.astype(f32), upstream).astype(jnp.bfloat16)
    grad_logits = (weights * (slope - lax.optimization_barrier(jnp.sum(weights * slope, axis=-1, keepdims=True))) * factor).astype(jnp.bfloat16)
    grad_query = jnp.einsum('chij,jchd->ichd', grad_logits.astype(f32), keys).astype(jnp.bfloat16)
    grad_keys = jnp.einsum('chij,ichd->jchd', grad_logits.astype(f32), query).astype(jnp.bfloat16)
    packed_grad = jnp.stack([grad_query, grad_keys, grad_values], axis=2).reshape(rows * cols, 3 * width)
    return (output, packed_grad)

def reference(row_query, row_key, row_value, column_weight, cotangent):
    f32 = jnp.float32
    scale = 1.0 / (math.sqrt(HEAD_DIM) * math.sqrt(DEPTH))

    def one_alignment(group):
        row_q, row_k, row_v, incoming = group
        query = row_q.astype(f32).reshape(DEPTH, COLUMNS, HEADS, HEAD_DIM)
        keys = row_k.astype(f32).reshape(DEPTH, COLUMNS, HEADS, HEAD_DIM)
        values = row_v.astype(f32).reshape(DEPTH, COLUMNS, HEADS, HEAD_DIM)
        scores = jnp.einsum('rihd,rjhd->hij', query, keys) * scale
        probs = jax.nn.softmax(scores, axis=-1)
        probs_low = probs.astype(jnp.bfloat16)
        hidden = jnp.einsum('hij,rjhd->rihd', probs_low.astype(f32), values).astype(jnp.bfloat16)
        hidden = hidden.reshape(DEPTH, COLUMNS, D)
        packed = jnp.dot(hidden.reshape(-1, D), column_weight, preferred_element_type=jnp.float32).astype(jnp.bfloat16)
        output, packed_grad = column_pass(hidden, packed, incoming)
        back = incoming.reshape(-1, D).astype(f32) + lax.dot_general(packed_grad, column_weight, (((1,), (1,)), ((), ())), preferred_element_type=jnp.float32)
        upstream = back.astype(jnp.bfloat16).astype(f32).reshape(DEPTH, COLUMNS, HEADS, HEAD_DIM)
        grad_value = jnp.einsum('hij,rihd->rjhd', probs_low.astype(f32), upstream).astype(jnp.bfloat16)
        slope = jnp.einsum('rihd,rjhd->hij', upstream, values)
        grad_scores = (probs * (slope - lax.optimization_barrier(jnp.sum(probs * slope, axis=-1, keepdims=True))) * scale).astype(jnp.bfloat16)
        grad_query = jnp.einsum('hij,rjhd->rihd', grad_scores.astype(f32), keys).astype(jnp.bfloat16)
        grad_key = jnp.einsum('hij,rihd->rjhd', grad_scores.astype(f32), query).astype(jnp.bfloat16)
        return (output, grad_query.reshape(DEPTH, COLUMNS, D), grad_key.reshape(DEPTH, COLUMNS, D), grad_value.reshape(DEPTH, COLUMNS, D))
    groups = tuple((x.reshape(N_GRP, DEPTH, COLUMNS, D) for x in (row_query, row_key, row_value, cotangent)))
    outputs, grad_q, grad_k, grad_v = lax.map(one_alignment, groups)
    total = N_GRP * DEPTH
    return (outputs.reshape(total, COLUMNS, D), grad_q.reshape(total, COLUMNS, D), grad_k.reshape(total, COLUMNS, D), grad_v.reshape(total, COLUMNS, D))
```

```python
import math

import jax
import jax.numpy as jnp
from jax import lax
from jax.sharding import PartitionSpec as P

HEADS = 12
HEAD_DIM = 64


def softmax_rows(logits):
    shifted = jnp.exp(logits - jnp.max(logits, axis=-1, keepdims=True))
    return shifted / jnp.sum(shifted, axis=-1, keepdims=True)


def column_pass(inputs, packed, incoming):
    f32 = jnp.float32
    rows, cols, width = inputs.shape
    packed = packed.reshape(rows, cols, 3, HEADS, HEAD_DIM)
    query = packed[:, :, 0]
    keys = packed[:, :, 1]
    values = packed[:, :, 2]
    factor = 1.0 / math.sqrt(HEAD_DIM)
    logits = jnp.einsum("ichd,jchd->chij", query, keys, preferred_element_type=f32) * factor
    weights = softmax_rows(logits)
    weights_low = weights.astype(jnp.bfloat16)
    attended = jnp.einsum("chij,jchd->ichd", weights_low, values, preferred_element_type=f32)
    output = (inputs.astype(f32) + attended.reshape(rows, cols, width)).astype(jnp.bfloat16)
    upstream = incoming.reshape(rows, cols, HEADS, HEAD_DIM)
    slope = jnp.einsum("ichd,jchd->chij", upstream, values, preferred_element_type=f32)
    grad_values = jnp.einsum(
        "chij,ichd->jchd", weights_low, upstream, preferred_element_type=f32
    ).astype(jnp.bfloat16)
    grad_logits = (
        weights * (slope - jnp.sum(weights * slope, axis=-1, keepdims=True)) * factor
    ).astype(jnp.bfloat16)
    grad_query = jnp.einsum(
        "chij,jchd->ichd", grad_logits, keys, preferred_element_type=f32
    ).astype(jnp.bfloat16)
    grad_keys = jnp.einsum(
        "chij,ichd->jchd", grad_logits, query, preferred_element_type=f32
    ).astype(jnp.bfloat16)
    packed_grad = jnp.stack([grad_query, grad_keys, grad_values], axis=2).reshape(
        rows * cols, 3 * width
    )
    return (output, packed_grad)


def scatter_sum(terms):
    heads, rows, cols = terms.shape
    members = lax.axis_size("seq")
    blocks = terms.reshape(heads, members, rows // members, cols).transpose(1, 0, 2, 3)
    received = lax.all_to_all(blocks, "seq", split_axis=0, concat_axis=0, tiled=True)
    return jnp.sum(received, axis=0)


def on_device(row_query, row_key, row_value, column_weight, cotangent):
    f32 = jnp.float32
    own_rows, columns, width = row_query.shape
    depth_rows = own_rows * lax.axis_size("seq")
    scale = 1.0 / (math.sqrt(HEAD_DIM) * math.sqrt(depth_rows))
    query = row_query.reshape(own_rows, columns, HEADS, HEAD_DIM)
    keys = row_key.reshape(own_rows, columns, HEADS, HEAD_DIM)
    values = row_value.reshape(own_rows, columns, HEADS, HEAD_DIM)
    local_scores = jnp.einsum("rihd,rjhd->hij", query, keys, preferred_element_type=f32)
    probs = softmax_rows(scatter_sum(local_scores) * scale)
    probs_low = lax.all_gather(probs.astype(jnp.bfloat16), "seq", axis=1, tiled=True)
    hidden = jnp.einsum("hij,rjhd->rihd", probs_low, values, preferred_element_type=f32)
    hidden = hidden.astype(jnp.bfloat16).reshape(own_rows, columns, width)
    column_inputs = lax.all_to_all(hidden, "seq", split_axis=1, concat_axis=0, tiled=True)
    block_rows, own_columns, _ = column_inputs.shape
    flat_inputs = column_inputs.reshape(block_rows * own_columns, width)
    full_weight = lax.all_gather(column_weight, "grp", axis=1, tiled=True)
    packed = jnp.dot(flat_inputs, full_weight, preferred_element_type=f32).astype(jnp.bfloat16)
    column_output, packed_grad = column_pass(column_inputs, packed, cotangent)
    incoming_flat = cotangent.reshape(block_rows * own_columns, width).astype(f32)
    back = incoming_flat + lax.dot_general(
        packed_grad, full_weight, (((1,), (1,)), ((), ())), preferred_element_type=f32
    )
    back = back.astype(jnp.bfloat16).reshape(block_rows, own_columns, width)
    upstream = lax.all_to_all(back, "seq", split_axis=0, concat_axis=1, tiled=True).reshape(
        own_rows, columns, HEADS, HEAD_DIM
    )
    grad_value = jnp.einsum(
        "hij,rihd->rjhd", probs_low, upstream, preferred_element_type=f32
    ).astype(jnp.bfloat16)
    local_slope = jnp.einsum("rihd,rjhd->hij", upstream, values, preferred_element_type=f32)
    slope = scatter_sum(local_slope)
    grad_scores = (probs * (slope - jnp.sum(probs * slope, axis=-1, keepdims=True)) * scale).astype(
        jnp.bfloat16
    )
    grad_scores = lax.all_gather(grad_scores, "seq", axis=1, tiled=True)
    grad_query = jnp.einsum("hij,rjhd->rihd", grad_scores, keys, preferred_element_type=f32).astype(
        jnp.bfloat16
    )
    grad_key = jnp.einsum("hij,rihd->rjhd", grad_scores, query, preferred_element_type=f32).astype(
        jnp.bfloat16
    )
    return (
        column_output,
        grad_query.reshape(own_rows, columns, width),
        grad_key.reshape(own_rows, columns, width),
        grad_value.reshape(own_rows, columns, width),
    )


def solution(mesh):
    in_specs = (
        P(("grp", "seq"), None, None),
        P(("grp", "seq"), None, None),
        P(("grp", "seq"), None, None),
        P(None, "grp"),
        P("grp", "seq", None),
    )
    out_specs = (
        P("grp", "seq", None),
        P(("grp", "seq"), None, None),
        P(("grp", "seq"), None, None),
        P(("grp", "seq"), None, None),
    )
    return jax.shard_map(
        on_device, mesh=mesh, in_specs=in_specs, out_specs=out_specs, check_vma=False
    )
```

```python
import functools
import math

import jax
import jax.numpy as jnp
from jax import lax
from jax.experimental import pallas as pl
from jax.experimental.pallas import tpu as pltpu
from jax.sharding import PartitionSpec as P

HEADS = 12
HEAD_DIM = 64
CHIPS = 16
SIDE = 4
HALF = 384
PAIRS = 3
MESH = pl.DeviceIdType.MESH
F32 = jnp.float32
BF16 = jnp.bfloat16

NN = (((1,), (0,)), ((), ()))
NT = (((1,), (1,)), ((), ()))
TN = (((0,), (0,)), ((), ()))


def dot(x, y, dims):
    return lax.dot_general(x, y, dims, preferred_element_type=F32)


def kernel(
    planes,
    q_in, k_in, v_in, w_in, cot_in,
    out, gq_out, gk_out, gv_out,
    qh, kh, vh, cot, weight, bias,
    s_send, s_recv, p_own, p_all, z_send, z_recv, abe, dabe, out_v,
    dz_send, dz_recv, dz_rows, g_send, g_recv, ds_all, gqh, gkh, gvh,
    local_sem, swap_send, swap_recv, ring_send, ring_recv, side_send, side_recv,
    s_ss, s_rs, p_ss, p_rs, z_ss, z_rs, dz_ss, dz_rs, g_ss, g_rs, ds_ss, ds_rs,
    back_send, back_recv,
):
    grp = lax.axis_index("grp")
    me = lax.axis_index("seq")
    chip = me // 2
    core = me % 2
    other = 1 - core
    chip_x, chip_y = chip % SIDE, chip // SIDE
    sibling = (grp, chip * 2 + other)
    above = (grp + 1) % planes
    below = (grp + planes - 1) % planes
    up_steps = planes // 2
    down_steps = (planes - 1) // 2
    scale = 1.0 / (math.sqrt(HEAD_DIM) * math.sqrt(4 * CHIPS))

    def target(k):
        return (chip_y + k // SIDE) % SIDE * SIDE + (chip_x + k % SIDE) % SIDE

    def source(k):
        return (chip_y + SIDE - k // SIDE) % SIDE * SIDE + (chip_x + SIDE - k % SIDE) % SIDE

    def remote(src, dst, send, recv, device):
        return pltpu.make_async_remote_copy(
            src_ref=src, dst_ref=dst, send_sem=send, recv_sem=recv,
            device_id=device, device_id_type=MESH,
        )

    barrier = pltpu.get_barrier_semaphore()

    @pl.loop(1, 2 * CHIPS)
    def _(k):
        pl.semaphore_signal(
            barrier, inc=1, device_id=(grp, (me + k) % (2 * CHIPS)), device_id_type=MESH
        )

    greeted = 2 * CHIPS - 1
    if up_steps:
        pl.semaphore_signal(barrier, inc=1, device_id=(above, me), device_id_type=MESH)
        pl.semaphore_signal(barrier, inc=1, device_id=(below, me), device_id_type=MESH)
        greeted += 2
    pl.semaphore_wait(barrier, greeted)

    mine = pl.ds(pl.multiple_of(core * HALF, HALF), HALF)
    theirs = pl.ds(pl.multiple_of(other * HALF, HALF), HALF)
    own_rows = pl.ds(core * 2, 2)
    their_rows = pl.ds(other * 2, 2)
    swaps, locals_ = [], []
    for n, (src, dst) in enumerate(((q_in, qh), (k_in, kh), (v_in, vh))):
        swaps.append(
            remote(src.at[:, :, theirs], dst.at[own_rows], swap_send.at[n], swap_recv.at[n], sibling)
        )
        locals_.append(
            pltpu.make_async_copy(src.at[:, :, mine], dst.at[own_rows], local_sem.at[n])
        )
    for n in range(3):
        swaps[n].start()
        locals_[n].start()

    def up_copy(step):
        block = (grp + planes - step) % planes
        src = w_in.at[:, mine] if step == 0 else weight.at[core, block]
        return remote(
            src, weight.at[core, block], ring_send.at[0, step], ring_recv.at[0, step], (above, me)
        )

    def down_copy(step):
        block = (grp + step) % planes
        src = w_in.at[:, mine] if step == 0 else weight.at[core, block]
        return remote(
            src, weight.at[core, block], ring_send.at[1, step], ring_recv.at[1, step], (below, me)
        )

    def side_copy(way, step):
        block = (grp + planes - step) % planes if way == 0 else (grp + step) % planes
        return remote(
            weight.at[core, block], weight.at[core, block],
            side_send.at[way, step], side_recv.at[way, step], sibling,
        )

    if up_steps:
        up_copy(0).start()
    if down_steps:
        down_copy(0).start()
    weight_own = [
        pltpu.make_async_copy(
            w_in.at[:, pl.ds(half * HALF, HALF)], weight.at[half, grp], local_sem.at[3 + half]
        )
        for half in range(2)
    ]
    for copy in weight_own:
        copy.start()
    cot_copy = pltpu.make_async_copy(cot_in, cot, local_sem.at[5])
    cot_copy.start()

    def ring(step):
        if step <= up_steps:
            up_copy(step - 1).wait_recv()
            if step < up_steps:
                up_copy(step).start()
            side_copy(0, step).start()
        if step <= down_steps:
            down_copy(step - 1).wait_recv()
            if step < down_steps:
                down_copy(step).start()
            side_copy(1, step).start()

    lane = lax.broadcasted_iota(jnp.int32, (1, 128), 1)
    low = jnp.where(lane < HEAD_DIM, 1.0, 0.0).astype(BF16)
    high = jnp.where(lane < HEAD_DIM, 0.0, 1.0).astype(BF16)
    low4 = jnp.concatenate([low] * 4, axis=1)
    high4 = jnp.concatenate([high] * 4, axis=1)
    row_id = lax.broadcasted_iota(jnp.int32, (256, 256), 0)
    col_id = lax.broadcasted_iota(jnp.int32, (256, 256), 1)
    bias[...] = jnp.where(row_id % 4 == col_id % 4, 0.0, -1e30)

    def wide(ref, t):
        return jnp.concatenate([ref[r, :, 128 * t : 128 * t + 128] for r in range(4)], axis=1)

    def terms(left, right, send_ref, t):
        for e, keep in enumerate((low4, high4)):
            h = 2 * t + e
            part = dot(left, right * keep, NT)
            send_ref[8 * (h // 3) : 8 * (h // 3) + 8, h % 3] = part.reshape(8, 16, 128)

    def gathered(ref, h):
        return ref[8 * (h // 3) : 8 * (h // 3) + 8, h % 3].reshape(128, 128)

    def scatter_copy(send_ref, recv_ref, ss, rs, to, slot):
        return remote(send_ref.at[to], recv_ref.at[slot], ss.at[to], rs.at[slot], (grp, to * 2 + core))

    def scatter_start(send_ref, recv_ref, ss, rs):
        @pl.loop(1, CHIPS)
        def _(k):
            scatter_copy(send_ref, recv_ref, ss, rs, target(k), chip).start()
        recv_ref[chip] = send_ref[chip]

    def scatter_wait(send_ref, recv_ref, ss, rs, first, last):
        @pl.loop(first, last)
        def _(k):
            scatter_copy(send_ref, recv_ref, ss, rs, target(k), source(k)).wait_recv()

    def gather_copy(ref, ss, rs, to, slot):
        return remote(ref.at[slot], ref.at[slot], ss.at[to], rs.at[slot], (grp, to * 2 + core))

    def gather_start(ref, ss, rs):
        @pl.loop(1, CHIPS)
        def _(k):
            gather_copy(ref, ss, rs, target(k), chip).start()

    def gather_wait(ref, ss, rs):
        @pl.loop(1, CHIPS)
        def _(k):
            gather_copy(ref, ss, rs, target(k), source(k)).wait_recv()

    for n in range(2):
        swaps[n].wait_recv()
        locals_[n].wait()
    for t in range(PAIRS):
        terms(wide(qh, t), wide(kh, t), s_send, t)
    scatter_start(s_send, s_recv, s_ss, s_rs)
    ring(1)
    scatter_wait(s_send, s_recv, s_ss, s_rs, 1, 8)
    ring(2)
    scatter_wait(s_send, s_recv, s_ss, s_rs, 8, CHIPS)
    scores = jnp.sum(s_recv[...], axis=0) * scale
    shifted = jnp.exp(scores - jnp.max(scores, axis=-1, keepdims=True))
    probs = shifted / jnp.sum(shifted, axis=-1, keepdims=True)
    p_own[...] = probs
    p_all[chip] = probs.astype(BF16)
    gather_start(p_all, p_ss, p_rs)
    ring(3)
    swaps[2].wait_recv()
    locals_[2].wait()
    gather_wait(p_all, p_ss, p_rs)
    ring(4)

    first4 = lax.broadcasted_iota(jnp.int32, (16, 8, 128), 1) < 4

    def interleave(x, y):
        lo = jnp.where(first4, x, pltpu.roll(y, 4, 1))
        hi = jnp.where(first4, pltpu.roll(x, 4, 1), y)
        return lo, hi

    for t in range(PAIRS):
        values = wide(vh, t)
        z = dot(gathered(p_all, 2 * t), values * low4, NN) + dot(
            gathered(p_all, 2 * t + 1), values * high4, NN
        )
        rows = [z[:, 128 * r : 128 * r + 128].reshape(16, 8, 128) for r in range(4)]
        lo01, hi01 = interleave(rows[0], rows[1])
        lo23, hi23 = interleave(rows[2], rows[3])
        lanes = slice(128 * t, 128 * t + 128)
        z_send[:, 0, :, lanes] = jnp.concatenate([lo01, lo23], axis=1).astype(BF16)
        z_send[:, 1, :, lanes] = jnp.concatenate([hi01, hi23], axis=1).astype(BF16)

    def z_copy(to, to_core, slot_core, slot):
        return remote(
            z_send.at[to, to_core], z_recv.at[slot_core, slot],
            z_ss.at[to, to_core], z_rs.at[slot_core, slot], (grp, to * 2 + to_core),
        )

    @pl.loop(1, CHIPS)
    def _(k):
        z_copy(target(k), core, core, chip).start()
        z_copy(target(k), other, core, chip).start()
    z_copy(chip, other, core, chip).start()
    z_recv[core, chip] = z_send[chip, core]

    for step in range(5, up_steps + 1):
        ring(step)

    for copy in weight_own:
        copy.wait()
    for step in range(1, up_steps + 1):
        side_copy(0, step).wait_recv()
    for step in range(1, down_steps + 1):
        side_copy(1, step).wait_recv()
    cot_copy.wait()

    z_copy(chip, other, other, chip).wait_recv()

    @pl.loop(1, CHIPS)
    def _(k):
        z_copy(target(k), core, core, source(k)).wait_recv()
        z_copy(target(k), other, other, source(k)).wait_recv()

    z0 = z_recv[0].reshape(256, HALF)
    z1 = z_recv[1].reshape(256, HALF)
    share = weight.shape[2]
    channels = planes * share
    for part in range(3):
        lo, hi = part * 768, part * 768 + 768
        w0 = weight[0].reshape(channels, HALF)[lo:hi]
        w1 = weight[1].reshape(channels, HALF)[lo:hi]
        packed = (dot(z0, w0, NT) + dot(z1, w1, NT)).astype(BF16)
        for u in range(6):
            abe[6 * part + u] = packed[:, 128 * u : 128 * u + 128]

    @pl.loop(0, 6)
    def _(u):
        lanes = pl.ds(pl.multiple_of(u * 128, 128), 128)
        half_lanes = pl.ds(pl.multiple_of((u % 3) * 128, 128), 128)
        a, b, e = abe[u], abe[6 + u], abe[12 + u]
        g = cot[:, lanes]
        att = z_recv[u // 3, :, :, half_lanes].reshape(256, 128).astype(F32)
        da = db = dc = None
        for keep in (low, high):
            ak, bk, ek, gk = a * keep, b * keep, e * keep, g * keep
            logits = dot(a, bk, NT) * 0.125 + bias[...]
            shifted = jnp.exp(logits - jnp.max(logits, axis=-1, keepdims=True))
            weights = shifted * (1.0 / jnp.sum(shifted, axis=-1, keepdims=True))
            weights_low = weights.astype(BF16)
            slope = dot(g, ek, NT)
            mean = jnp.sum(weights * slope, axis=-1, keepdims=True)
            dlogits = (weights * (slope - mean) * 0.125).astype(BF16)
            att = att + dot(weights_low, ek, NN)
            terms_ = (dot(dlogits, bk, NN), dot(dlogits, ak, TN), dot(weights_low, gk, TN))
            if da is None:
                da, db, dc = terms_
            else:
                da, db, dc = da + terms_[0], db + terms_[1], dc + terms_[2]
        out_v[:, lanes] = att.astype(BF16)
        dabe[u] = da.astype(BF16)
        dabe[6 + u] = db.astype(BF16)
        dabe[12 + u] = dc.astype(BF16)

    out_copy = pltpu.make_async_copy(out_v, out, local_sem.at[6])
    out_copy.start()

    def dz_copy(to, to_core, slot, slot_core):
        return remote(
            dz_send.at[to_core, to], dz_recv.at[slot, slot_core],
            dz_ss.at[to_core, to], dz_rs.at[slot, slot_core], (grp, to * 2 + to_core),
        )

    dpacked = jnp.concatenate([dabe[n] for n in range(18)], axis=1)
    for half in range(2):
        back = cot[:, half * HALF : half * HALF + HALF].astype(F32) + dot(
            dpacked, weight[half].reshape(channels, HALF), NN
        )
        dz_send[half] = back.astype(BF16).reshape(16, 16, HALF)

    @pl.loop(1, CHIPS)
    def _(k):
        dz_copy(target(k), core, chip, core).start()
        dz_copy(target(k), other, chip, core).start()
    dz_copy(chip, other, chip, core).start()
    dz_recv[chip, core] = dz_send[core, chip]

    dz_copy(chip, other, chip, other).wait_recv()

    @pl.loop(1, CHIPS)
    def _(k):
        dz_copy(target(k), core, source(k), core).wait_recv()
        dz_copy(target(k), other, source(k), other).wait_recv()

    for t in range(PAIRS):
        lanes = slice(128 * t, 128 * t + 128)
        even = dz_recv[:, 0, :, lanes].astype(F32)
        odd = dz_recv[:, 1, :, lanes].astype(F32)
        r0, r1 = interleave(even[:, :8], odd[:, :8])
        r2, r3 = interleave(even[:, 8:], odd[:, 8:])
        dz = jnp.concatenate(
            [x.reshape(128, 128).astype(BF16) for x in (r0, r1, r2, r3)], axis=1
        )
        dz_rows[t] = dz
        terms(dz, wide(vh, t), g_send, t)
    scatter_start(g_send, g_recv, g_ss, g_rs)

    def store(ref, t, x):
        for r in range(4):
            ref[r, :, 128 * t : 128 * t + 128] = x[:, 128 * r : 128 * r + 128].astype(BF16)

    def give_back(ref, out_ref, n):
        local = pltpu.make_async_copy(ref.at[own_rows], out_ref.at[:, :, mine], local_sem.at[7 + n])
        away = remote(
            ref.at[their_rows], out_ref.at[:, :, mine], back_send.at[n], back_recv.at[n], sibling
        )
        landing = remote(
            ref.at[their_rows], out_ref.at[:, :, theirs], back_send.at[n], back_recv.at[n], sibling
        )
        local.start()
        away.start()
        return local, away, landing

    for t in range(PAIRS):
        dz = dz_rows[t]
        store(gvh, t, dot(gathered(p_all, 2 * t), dz * low4, TN)
              + dot(gathered(p_all, 2 * t + 1), dz * high4, TN))
    returned = [give_back(gvh, gv_out, 0)]

    scatter_wait(g_send, g_recv, g_ss, g_rs, 1, CHIPS)
    slope = jnp.sum(g_recv[...], axis=0)
    probs = p_own[...]
    mean = jnp.sum(probs * slope, axis=-1, keepdims=True)
    ds_all[chip] = (probs * (slope - mean) * scale).astype(BF16)
    gather_start(ds_all, ds_ss, ds_rs)
    gather_wait(ds_all, ds_ss, ds_rs)
    for t in range(PAIRS):
        keys = wide(kh, t)
        store(gqh, t, dot(gathered(ds_all, 2 * t), keys * low4, NN)
              + dot(gathered(ds_all, 2 * t + 1), keys * high4, NN))
    returned.append(give_back(gqh, gq_out, 1))
    for t in range(PAIRS):
        query = wide(qh, t)
        store(gkh, t, dot(gathered(ds_all, 2 * t), query * low4, TN)
              + dot(gathered(ds_all, 2 * t + 1), query * high4, TN))
    returned.append(give_back(gkh, gk_out, 2))

    for copy in swaps:
        copy.wait_send()
    for step in range(up_steps):
        up_copy(step).wait_send()
        side_copy(0, step + 1).wait_send()
    for step in range(down_steps):
        down_copy(step).wait_send()
        side_copy(1, step + 1).wait_send()

    @pl.loop(1, CHIPS)
    def _(k):
        to = target(k)
        scatter_copy(s_send, s_recv, s_ss, s_rs, to, chip).wait_send()
        gather_copy(p_all, p_ss, p_rs, to, chip).wait_send()
        z_copy(to, core, core, chip).wait_send()
        z_copy(to, other, core, chip).wait_send()
        dz_copy(to, core, chip, core).wait_send()
        dz_copy(to, other, chip, core).wait_send()
        scatter_copy(g_send, g_recv, g_ss, g_rs, to, chip).wait_send()
        gather_copy(ds_all, ds_ss, ds_rs, to, chip).wait_send()
    z_copy(chip, other, core, chip).wait_send()
    dz_copy(chip, other, chip, core).wait_send()
    out_copy.wait()
    for local, away, landing in returned:
        local.wait()
        away.wait_send()
        landing.wait_recv()


def on_device(planes, row_query, row_key, row_value, column_weight, cotangent):
    own_rows, columns, width = row_query.shape
    share = column_weight.shape[1]
    rows, own_columns, _ = cotangent.shape
    vmem = pltpu.VMEM
    sem = pltpu.SemaphoreType.DMA
    row_shape = jax.ShapeDtypeStruct((own_rows, columns, width), BF16)
    column_output, grad_query, grad_key, grad_value = pl.pallas_call(
        functools.partial(kernel, planes),
        out_shape=(
            jax.ShapeDtypeStruct((rows * own_columns, width), BF16),
            row_shape, row_shape, row_shape,
        ),
        in_specs=[pl.BlockSpec(memory_space=pl.ANY)] * 5,
        out_specs=[pl.BlockSpec(memory_space=pl.ANY)] * 4,
        scratch_shapes=[
            vmem((4, 128, HALF), BF16),
            vmem((4, 128, HALF), BF16),
            vmem((4, 128, HALF), BF16),
            vmem((256, 768), BF16),
            vmem((2, planes, share, HALF), BF16),
            vmem((256, 256), F32),
            vmem((CHIPS, 3, 16, 128), F32),
            vmem((CHIPS, 3, 16, 128), F32),
            vmem((3, 16, 128), F32),
            vmem((CHIPS, 3, 16, 128), BF16),
            vmem((CHIPS, 2, 16, HALF), BF16),
            vmem((2, CHIPS, 16, HALF), BF16),
            vmem((18, 256, 128), BF16),
            vmem((18, 256, 128), BF16),
            vmem((256, 768), BF16),
            vmem((2, CHIPS, 16, HALF), BF16),
            vmem((CHIPS, 2, 16, HALF), BF16),
            vmem((PAIRS, 128, 512), BF16),
            vmem((CHIPS, 3, 16, 128), F32),
            vmem((CHIPS, 3, 16, 128), F32),
            vmem((CHIPS, 3, 16, 128), BF16),
            vmem((4, 128, HALF), BF16),
            vmem((4, 128, HALF), BF16),
            vmem((4, 128, HALF), BF16),
            sem((10,)),
            sem((3,)), sem((3,)),
            sem((2, planes)), sem((2, planes)),
            sem((2, planes)), sem((2, planes)),
            sem((CHIPS,)), sem((CHIPS,)),
            sem((CHIPS,)), sem((CHIPS,)),
            sem((CHIPS, 2)), sem((2, CHIPS)),
            sem((2, CHIPS)), sem((CHIPS, 2)),
            sem((CHIPS,)), sem((CHIPS,)),
            sem((CHIPS,)), sem((CHIPS,)),
            sem((3,)), sem((3,)),
        ],
        compiler_params=pltpu.CompilerParams(
            collective_id=0, has_side_effects=True, vmem_limit_bytes=48 * 1024 * 1024
        ),
    )(
        row_query, row_key, row_value, column_weight.T,
        cotangent.reshape(rows * own_columns, width),
    )
    return (
        column_output.reshape(rows, own_columns, width), grad_query, grad_key, grad_value
    )


def solution(mesh):
    planes = mesh.shape["grp"]
    in_specs = (
        P(("grp", "seq"), None, None),
        P(("grp", "seq"), None, None),
        P(("grp", "seq"), None, None),
        P(None, "grp"),
        P("grp", "seq", None),
    )
    out_specs = (
        P("grp", "seq", None),
        P(("grp", "seq"), None, None),
        P(("grp", "seq"), None, None),
        P(("grp", "seq"), None, None),
    )
    return jax.shard_map(
        functools.partial(on_device, planes),
        mesh=mesh, in_specs=in_specs, out_specs=out_specs, check_vma=False,
    )
```

```python
import functools
import math

import jax
import jax.numpy as jnp
from jax import lax
from jax.experimental import pallas as pl
from jax.experimental.pallas import tpu as pltpu
from jax.sharding import PartitionSpec as P

HEADS = 12
HEAD_DIM = 64
CHIPS = 16
SIDE = 4
HALF = 384
PAIRS = 3
MESH = pl.DeviceIdType.MESH
VMEM_LIMIT = 60 * 1024 * 1024
F32 = jnp.float32
BF16 = jnp.bfloat16

NN = (((1,), (0,)), ((), ()))
NT = (((1,), (1,)), ((), ()))
TN = (((0,), (0,)), ((), ()))


def dot(x, y, dims):
    return lax.dot_general(x, y, dims, preferred_element_type=F32)


def copy_out(*refs):
    sources, targets, sem = refs[:4], refs[4:8], refs[8]
    copies = [pltpu.make_async_copy(sources[n], targets[n], sem.at[n]) for n in range(4)]
    for copy in copies:
        copy.start()
    for copy in copies:
        copy.wait()


def kernel(
    planes,
    q_in, k_in, v_in, w_in, cot_in,
    out, gq_out, gk_out, gv_out,
    qh, kh, vh, cot4, cot, weight, bias,
    s_send, s_recv, p_own, p_all, z_send, z_recv, zh, abe, dabe, outh, out4,
    dz_send, dz_recv, dz_rows, g_send, g_recv, ds_all, gqh, gkh, gvh,
    local_sem, swap_send, swap_recv, ring_send, ring_recv, side_send, side_recv,
    many_send, many_recv, back_send, back_recv,
):
    grp = lax.axis_index("grp")
    me = lax.axis_index("seq")
    chip = lax.div(me, 2)
    core = lax.rem(me, 2)
    other = 1 - core
    chip_x, chip_y = lax.rem(chip, SIDE), lax.div(chip, SIDE)
    sibling = (grp, chip * 2 + other)
    above = lax.rem(grp + 1, planes)
    below = lax.rem(grp + planes - 1, planes)
    up_steps = planes // 2
    down_steps = (planes - 1) // 2
    scale = 1.0 / (math.sqrt(HEAD_DIM) * math.sqrt(4 * CHIPS))

    targets = [None] + [
        lax.rem(chip_y + k // SIDE, SIDE) * SIDE + lax.rem(chip_x + k % SIDE, SIDE)
        for k in range(1, CHIPS)
    ]

    def remote(src, dst, send, recv, device):
        return pltpu.make_async_remote_copy(
            src_ref=src, dst_ref=dst, send_sem=send, recv_sem=recv,
            device_id=device, device_id_type=MESH,
        )

    barrier = pltpu.get_barrier_semaphore()

    @pl.loop(1, 2 * CHIPS)
    def _(k):
        pl.semaphore_signal(
            barrier, inc=1, device_id=(grp, lax.rem(me + k, 2 * CHIPS)), device_id_type=MESH
        )

    greeted = 2 * CHIPS - 1
    if up_steps:
        pl.semaphore_signal(barrier, inc=1, device_id=(above, me), device_id_type=MESH)
        pl.semaphore_signal(barrier, inc=1, device_id=(below, me), device_id_type=MESH)
        greeted += 2
    pl.semaphore_wait(barrier, greeted)

    mine = pl.ds(pl.multiple_of(core * HALF, HALF), HALF)
    theirs = pl.ds(pl.multiple_of(other * HALF, HALF), HALF)
    own_rows = pl.ds(core * 2, 2)
    their_rows = pl.ds(other * 2, 2)
    swaps, locals_ = [], []
    for n, (src, dst) in enumerate(((q_in, qh), (k_in, kh), (v_in, vh))):
        swaps.append(
            remote(src.at[:, :, theirs], dst.at[own_rows], swap_send.at[n], swap_recv.at[n], sibling)
        )
        locals_.append(
            pltpu.make_async_copy(src.at[:, :, mine], dst.at[own_rows], local_sem.at[n])
        )
    for n in range(3):
        swaps[n].start()
        locals_[n].start()

    share = w_in.shape[0]
    first = (share // 16 + 1) // 2 * 16
    cuts = ((0, first), (first, share - first))

    def block_rows(way, step):
        block = lax.rem(grp + planes - step, planes) if way == 0 else lax.rem(grp + step, planes)
        return pl.multiple_of(block * share, 16)

    def ring_copy(way, step, part):
        begin, size = cuts[part]
        rows = pl.ds(pl.multiple_of(block_rows(way, step) + begin, 16), size)
        src = w_in.at[pl.ds(begin, size), mine] if step == 0 else weight.at[core, rows]
        return remote(
            src, weight.at[core, rows], ring_send.at[way, step, part],
            ring_recv.at[way, step, part], (below if way else above, me),
        )

    def side_copy(way, step):
        rows = weight.at[core, pl.ds(block_rows(way, step), share)]
        return remote(rows, rows, side_send.at[way, step], side_recv.at[way, step], sibling)

    for part in range(2):
        if up_steps:
            ring_copy(0, 0, part).start()
        if down_steps:
            ring_copy(1, 0, part).start()
    weight_own = [
        pltpu.make_async_copy(
            w_in.at[:, pl.ds(half * HALF, HALF)],
            weight.at[half, pl.ds(block_rows(0, 0), share)], local_sem.at[3 + half],
        )
        for half in range(2)
    ]
    for copy in weight_own:
        copy.start()
    cot_copy = pltpu.make_async_copy(cot_in, cot4, local_sem.at[5])
    cot_copy.start()

    def ring(first_turn, last_turn):
        for turn in range(first_turn, last_turn):
            step, part = turn // 2 + 1, turn % 2
            for way, steps in enumerate((up_steps, down_steps)):
                if step <= steps:
                    ring_copy(way, step - 1, part).wait_recv()
                    if step < steps:
                        ring_copy(way, step, part).start()
                    if part == 1:
                        side_copy(way, step).start()

    lane = lax.broadcasted_iota(jnp.int32, (1, 128), 1)
    low = jnp.where(lane < HEAD_DIM, 1.0, 0.0).astype(BF16)
    high = jnp.where(lane < HEAD_DIM, 0.0, 1.0).astype(BF16)
    low4 = jnp.concatenate([low] * 4, axis=1)
    high4 = jnp.concatenate([high] * 4, axis=1)
    row_id = lax.broadcasted_iota(jnp.int32, (128, 128), 0)
    col_id = lax.broadcasted_iota(jnp.int32, (128, 128), 1)
    bias[...] = jnp.where(row_id % 2 == col_id % 2, 0.0, -1e30)

    def wide(ref, t):
        return jnp.concatenate([ref[r, :, 128 * t : 128 * t + 128] for r in range(4)], axis=1)

    def terms(left, right, send_ref, t):
        for e, keep in enumerate((low4, high4)):
            h = 2 * t + e
            part = dot(left, right * keep, NT)
            send_ref[8 * (h // 3) : 8 * (h // 3) + 8, h % 3] = part.reshape(8, 16, 128)

    def gathered(ref, h):
        return ref[8 * (h // 3) : 8 * (h // 3) + 8, h % 3].reshape(128, 128)

    def scatter(send_ref, recv_ref, n):
        for k in range(1, CHIPS):
            to = targets[k]
            remote(
                send_ref.at[to], recv_ref.at[chip], many_send.at[n], many_recv.at[n],
                (grp, to * 2 + core),
            ).start()
        recv_ref[chip] = send_ref[chip]
        rest = pl.ds(0, CHIPS - 1)
        return remote(
            send_ref.at[rest], recv_ref.at[rest], many_send.at[n], many_recv.at[n], sibling
        )

    def gather(ref, n):
        for k in range(1, CHIPS):
            remote(
                ref.at[chip], ref.at[chip], many_send.at[n], many_recv.at[n],
                (grp, targets[k] * 2 + core),
            ).start()
        rest = pl.ds(0, CHIPS - 1)
        return remote(ref.at[rest], ref.at[rest], many_send.at[n], many_recv.at[n], sibling)

    def exchange(send_ref, recv_ref, n):
        for k in range(1, CHIPS):
            for to in (targets[k] * 2 + core, targets[k] * 2 + other):
                remote(
                    send_ref.at[to], recv_ref.at[me], many_send.at[n], many_recv.at[n], (grp, to)
                ).start()
        remote(
            send_ref.at[chip * 2 + other], recv_ref.at[me], many_send.at[n], many_recv.at[n],
            sibling,
        ).start()
        recv_ref[me] = send_ref[me]
        rest = pl.ds(0, 2 * CHIPS - 1)
        return remote(
            send_ref.at[rest], recv_ref.at[rest], many_send.at[n], many_recv.at[n], sibling
        )

    sublane = lax.broadcasted_iota(jnp.int32, (16, 8, 128), 1)
    first4 = sublane < 4
    first2 = lax.rem(sublane, 4) < 2

    def swap4(x, y):
        return jnp.where(first4, x, pltpu.roll(y, 4, 1)), jnp.where(first4, pltpu.roll(x, 4, 1), y)

    def swap2(x, y):
        return jnp.where(first2, x, pltpu.roll(y, 2, 1)), jnp.where(first2, pltpu.roll(x, 6, 1), y)

    for n in range(2):
        swaps[n].wait_recv()
        locals_[n].wait()
    for t in range(PAIRS):
        terms(wide(qh, t), wide(kh, t), s_send, t)
    s_all = scatter(s_send, s_recv, 0)
    ring(0, 3)
    s_all.wait_recv()
    scores = jnp.sum(s_recv[...], axis=0) * scale
    shifted = jnp.exp(scores - jnp.max(scores, axis=-1, keepdims=True))
    probs = shifted / jnp.sum(shifted, axis=-1, keepdims=True)
    p_own[...] = probs
    p_all[chip] = probs.astype(BF16)
    p_rest = gather(p_all, 1)
    ring(3, 6)
    cot_copy.wait()
    for u in range(6):
        lanes = slice(128 * u, 128 * u + 128)
        g4 = cot4[:, :, lanes].astype(F32)
        for c in range(2):
            cot[c, :, lanes] = g4[:, 2 * c : 2 * c + 2].reshape(128, 128).astype(BF16)
    swaps[2].wait_recv()
    locals_[2].wait()
    p_rest.wait_recv()

    for t in range(PAIRS):
        values = wide(vh, t)
        z = dot(gathered(p_all, 2 * t), values * low4, NN) + dot(
            gathered(p_all, 2 * t + 1), values * high4, NN
        )
        rows = [z[:, 128 * r : 128 * r + 128].reshape(16, 8, 128) for r in range(4)]
        lanes = slice(128 * t, 128 * t + 128)
        for c, (x, y) in enumerate(zip(swap4(rows[0], rows[2]), swap4(rows[1], rows[3]))):
            block = jnp.concatenate(swap2(x, y), axis=1).astype(BF16)
            for n in range(CHIPS):
                z_send[2 * n + c, :, lanes] = block[n]
    z_rest = exchange(z_send, z_recv, 2)
    ring(6, 2 * up_steps)

    for copy in weight_own:
        copy.wait()
    for step in range(1, up_steps + 1):
        side_copy(0, step).wait_recv()
    for step in range(1, down_steps + 1):
        side_copy(1, step).wait_recv()
    z_rest.wait_recv()

    arrived = z_recv[...].reshape(CHIPS, 2, 16, HALF)
    for half in range(2):
        for t in range(PAIRS):
            z = arrived[:, half, :, 128 * t : 128 * t + 128].astype(F32)
            lanes = slice(half * HALF + 128 * t, half * HALF + 128 * t + 128)
            for c in range(2):
                zh[128 * c : 128 * c + 128, lanes] = (
                    z[:, 8 * c : 8 * c + 8].reshape(128, 128).astype(BF16)
                )
    for part in range(3):
        rows = slice(part * 768, part * 768 + 768)
        w = jnp.concatenate([weight[0, rows], weight[1, rows]], axis=1)
        packed = dot(zh[...], w, NT).astype(BF16)
        for u in range(6):
            abe[6 * part + u] = packed[:, 128 * u : 128 * u + 128]

    @pl.loop(0, 6)
    def _(u):
        lanes = pl.ds(pl.multiple_of(u * 128, 128), 128)
        for c in range(2):
            rows = slice(128 * c, 128 * c + 128)
            a, b, e = abe[u, rows], abe[6 + u, rows], abe[12 + u, rows]
            g = cot[c, :, lanes]
            att = zh[rows, lanes].astype(F32)
            sums = None
            for keep in (low, high):
                ak, bk, ek, gk = a * keep, b * keep, e * keep, g * keep
                logits = dot(a, bk, NT) * 0.125 + bias[...]
                shifted = jnp.exp(logits - jnp.max(logits, axis=-1, keepdims=True))
                weights = shifted * (1.0 / jnp.sum(shifted, axis=-1, keepdims=True))
                weights_low = weights.astype(BF16)
                slope = dot(g, ek, NT)
                mean = jnp.sum(weights * slope, axis=-1, keepdims=True)
                dlogits = (weights * (slope - mean) * 0.125).astype(BF16)
                att = att + dot(weights_low, ek, NN)
                parts = (dot(dlogits, bk, NN), dot(dlogits, ak, TN), dot(weights_low, gk, TN))
                sums = parts if sums is None else [x + y for x, y in zip(sums, parts)]
            outh[c, :, lanes] = att.astype(BF16)
            for n in range(3):
                dabe[6 * n + u, rows] = sums[n].astype(BF16)

    dpacked = jnp.concatenate([dabe[n] for n in range(18)], axis=1)
    for half in range(2):
        lanes = slice(half * HALF, half * HALF + HALF)
        back = dot(dpacked, weight[half], NN)
        blocks = jnp.concatenate(
            [
                (cot[c, :, lanes].astype(F32) + back[128 * c : 128 * c + 128]).reshape(16, 8, HALF)
                for c in range(2)
            ],
            axis=1,
        ).astype(BF16)
        for n in range(CHIPS):
            dz_send[2 * n + half] = blocks[n]
    dz_rest = exchange(dz_send, dz_recv, 3)

    for u in range(6):
        lanes = slice(128 * u, 128 * u + 128)
        out4[:, :, lanes] = jnp.concatenate(
            [outh[c, :, lanes].astype(F32).reshape(64, 2, 128) for c in range(2)], axis=1
        ).astype(BF16)
    out_copy = pltpu.make_async_copy(out4, out, local_sem.at[6])
    out_copy.start()
    for copy in swaps:
        copy.wait_send()
    for way, steps in enumerate((up_steps, down_steps)):
        for step in range(steps):
            for part in range(2):
                ring_copy(way, step, part).wait_send()
            side_copy(way, step + 1).wait_send()
    for rest in (s_all, p_rest, z_rest):
        rest.wait_send()
    dz_rest.wait_recv()

    for t in range(PAIRS):
        lanes = slice(128 * t, 128 * t + 128)
        blocks = dz_recv[...].reshape(CHIPS, 2, 16, HALF)[:, :, :, lanes].astype(F32)
        x02, x13 = zip(*[swap2(blocks[:, c, :8], blocks[:, c, 8:]) for c in range(2)])
        r0, r2 = swap4(*x02)
        r1, r3 = swap4(*x13)
        dz = jnp.concatenate(
            [x.reshape(128, 128).astype(BF16) for x in (r0, r1, r2, r3)], axis=1
        )
        dz_rows[t] = dz
        terms(dz, wide(vh, t), g_send, t)
    g_rest = scatter(g_send, g_recv, 4)

    def store(ref, t, x):
        for r in range(4):
            ref[r, :, 128 * t : 128 * t + 128] = x[:, 128 * r : 128 * r + 128].astype(BF16)

    def give_back(ref, out_ref, n):
        local = pltpu.make_async_copy(ref.at[own_rows], out_ref.at[:, :, mine], local_sem.at[7 + n])
        away = remote(
            ref.at[their_rows], out_ref.at[:, :, mine], back_send.at[n], back_recv.at[n], sibling
        )
        landing = remote(
            ref.at[their_rows], out_ref.at[:, :, theirs], back_send.at[n], back_recv.at[n], sibling
        )
        local.start()
        away.start()
        return local, away, landing

    for t in range(PAIRS):
        dz = dz_rows[t]
        store(gvh, t, dot(gathered(p_all, 2 * t), dz * low4, TN)
              + dot(gathered(p_all, 2 * t + 1), dz * high4, TN))
    returned = [give_back(gvh, gv_out, 0)]

    dz_rest.wait_send()
    g_rest.wait_recv()
    slope = jnp.sum(g_recv[...], axis=0)
    probs = p_own[...]
    mean = jnp.sum(probs * slope, axis=-1, keepdims=True)
    ds_all[chip] = (probs * (slope - mean) * scale).astype(BF16)
    ds_rest = gather(ds_all, 5)
    out_copy.wait()
    g_rest.wait_send()
    ds_rest.wait_recv()
    for t in range(PAIRS):
        keys = wide(kh, t)
        store(gqh, t, dot(gathered(ds_all, 2 * t), keys * low4, NN)
              + dot(gathered(ds_all, 2 * t + 1), keys * high4, NN))
    returned.append(give_back(gqh, gq_out, 1))
    for t in range(PAIRS):
        query = wide(qh, t)
        store(gkh, t, dot(gathered(ds_all, 2 * t), query * low4, TN)
              + dot(gathered(ds_all, 2 * t + 1), query * high4, TN))
    returned.append(give_back(gkh, gk_out, 2))

    ds_rest.wait_send()
    for local, away, landing in returned:
        local.wait()
        away.wait_send()
        landing.wait_recv()


def on_device(planes, row_query, row_key, row_value, column_weight, cotangent):
    own_rows, columns, width = row_query.shape
    share = column_weight.shape[1]
    rows, own_columns, _ = cotangent.shape
    vmem = pltpu.VMEM
    sem = pltpu.SemaphoreType.DMA
    row_shape = jax.ShapeDtypeStruct((own_rows, columns, width), BF16)
    shapes = (jax.ShapeDtypeStruct(cotangent.shape, BF16), row_shape, row_shape, row_shape)
    results = pl.pallas_call(
        functools.partial(kernel, planes),
        out_shape=shapes,
        in_specs=[pl.BlockSpec(memory_space=pl.ANY)] * 5,
        out_specs=[pl.BlockSpec(memory_space=pl.ANY)] * 4,
        scratch_shapes=[
            vmem((4, 128, HALF), BF16),
            vmem((4, 128, HALF), BF16),
            vmem((4, 128, HALF), BF16),
            vmem((rows, own_columns, width), BF16),
            vmem((2, 128, 768), BF16),
            vmem((2, planes * share, HALF), BF16),
            vmem((128, 128), F32),
            vmem((CHIPS, 3, 16, 128), F32),
            vmem((CHIPS, 3, 16, 128), F32),
            vmem((3, 16, 128), F32),
            vmem((CHIPS, 3, 16, 128), BF16),
            vmem((2 * CHIPS, 16, HALF), BF16),
            vmem((2 * CHIPS, 16, HALF), BF16),
            vmem((256, 768), BF16),
            vmem((18, 256, 128), BF16),
            vmem((18, 256, 128), BF16),
            vmem((2, 128, 768), BF16),
            vmem((rows, own_columns, width), BF16),
            vmem((2 * CHIPS, 16, HALF), BF16),
            vmem((2 * CHIPS, 16, HALF), BF16),
            vmem((PAIRS, 128, 512), BF16),
            vmem((CHIPS, 3, 16, 128), F32),
            vmem((CHIPS, 3, 16, 128), F32),
            vmem((CHIPS, 3, 16, 128), BF16),
            vmem((4, 128, HALF), BF16),
            vmem((4, 128, HALF), BF16),
            vmem((4, 128, HALF), BF16),
            sem((10,)),
            sem((3,)), sem((3,)),
            sem((2, planes, 2)), sem((2, planes, 2)),
            sem((2, planes)), sem((2, planes)),
            sem((6,)), sem((6,)),
            sem((3,)), sem((3,)),
        ],
        compiler_params=pltpu.CompilerParams(
            collective_id=0, has_side_effects=True, vmem_limit_bytes=VMEM_LIMIT
        ),
    )(row_query, row_key, row_value, column_weight.T, cotangent)
    return pl.pallas_call(
        copy_out,
        out_shape=shapes,
        in_specs=[pl.BlockSpec(memory_space=pl.ANY)] * 4,
        out_specs=[pl.BlockSpec(memory_space=pl.ANY)] * 4,
        scratch_shapes=[sem((4,))],
        compiler_params=pltpu.CompilerParams(vmem_limit_bytes=VMEM_LIMIT),
    )(*results)


def solution(mesh):
    planes = mesh.shape["grp"]
    in_specs = (
        P(("grp", "seq"), None, None),
        P(("grp", "seq"), None, None),
        P(("grp", "seq"), None, None),
        P(None, "grp"),
        P("grp", "seq", None),
    )
    out_specs = (
        P("grp", "seq", None),
        P(("grp", "seq"), None, None),
        P(("grp", "seq"), None, None),
        P(("grp", "seq"), None, None),
    )
    return jax.shard_map(
        functools.partial(on_device, planes),
        mesh=mesh, in_specs=in_specs, out_specs=out_specs, check_vma=False,
    )
```

```python
import functools
import math

import jax
import jax.numpy as jnp
from jax import lax
from jax.experimental import pallas as pl
from jax.experimental.pallas import tpu as pltpu
from jax.sharding import PartitionSpec as P

HEADS = 12
HEAD_DIM = 64
CHIPS = 16
SIDE = 4
HALF = 384
PAIRS = 3
MESH = pl.DeviceIdType.MESH
VMEM_LIMIT = 60 * 1024 * 1024
F32 = jnp.float32
BF16 = jnp.bfloat16

NN = (((1,), (0,)), ((), ()))
NT = (((1,), (1,)), ((), ()))
TN = (((0,), (0,)), ((), ()))


def dot(x, y, dims):
    return lax.dot_general(x, y, dims, preferred_element_type=F32)


def copy_out(*refs):
    sources, targets, held, in_sem, out_sem = refs[:4], refs[4:8], refs[8:12], refs[12], refs[13]
    pieces = []
    for n in range(4):
        half = sources[n].shape[0] // 2
        for m in range(2):
            rows = pl.ds(m * half, half)
            pieces.append((
                pltpu.make_async_copy(sources[n].at[rows], held[n].at[rows], in_sem.at[2 * n + m]),
                pltpu.make_async_copy(held[n].at[rows], targets[n].at[rows], out_sem.at[2 * n + m]),
            ))
    for arrive, _ in pieces:
        arrive.start()
    for arrive, leave in pieces:
        arrive.wait()
        leave.start()
    for _, leave in pieces:
        leave.wait()


def kernel(
    planes,
    q_in, k_in, v_in, w_in, cot_in,
    out, gq_out, gk_out, gv_out,
    qh, kh, vh, cot4, cot, weight, bias,
    s_send, s_recv, p_own, p_all, z_send, z_recv, zh, abe, dabe, outh, out4,
    dz_send, dz_recv, dz_rows, g_send, g_recv, ds_all, gqh, gkh, gvh,
    local_sem, swap_send, swap_recv, ring_send, ring_recv, side_send, side_recv,
    many_send, many_recv, back_send, back_recv,
):
    grp = lax.axis_index("grp")
    me = lax.axis_index("seq")
    chip = lax.div(me, 2)
    core = lax.rem(me, 2)
    other = 1 - core
    chip_x, chip_y = lax.rem(chip, SIDE), lax.div(chip, SIDE)
    sibling = (grp, chip * 2 + other)
    far = planes // 2
    reach = (far, planes - 1 - far)

    def plane(step):
        return lax.rem(grp + planes + step, planes)

    scale = 1.0 / (math.sqrt(HEAD_DIM) * math.sqrt(4 * CHIPS))

    def hops(k):
        return min(k % SIDE, SIDE - k % SIDE) + min(k // SIDE, SIDE - k // SIDE)

    targets = [
        lax.rem(chip_y + k // SIDE, SIDE) * SIDE + lax.rem(chip_x + k % SIDE, SIDE)
        for k in sorted(range(1, CHIPS), key=lambda k: -hops(k))
    ]

    def remote(src, dst, send, recv, device):
        return pltpu.make_async_remote_copy(
            src_ref=src, dst_ref=dst, send_sem=send, recv_sem=recv,
            device_id=device, device_id_type=MESH,
        )

    barrier = pltpu.get_barrier_semaphore()

    @pl.loop(1, 2 * CHIPS)
    def _(k):
        pl.semaphore_signal(
            barrier, inc=1, device_id=(grp, lax.rem(me + k, 2 * CHIPS)), device_id_type=MESH
        )

    near = (-2, -1, 1, 2)
    for step in near:
        pl.semaphore_signal(barrier, inc=1, device_id=(plane(step), me), device_id_type=MESH)
    pl.semaphore_wait(barrier, 2 * CHIPS - 1 + len(near))

    mine = pl.ds(pl.multiple_of(core * HALF, HALF), HALF)
    theirs = pl.ds(pl.multiple_of(other * HALF, HALF), HALF)
    own_rows = pl.ds(core * 2, 2)
    their_rows = pl.ds(other * 2, 2)
    swaps, locals_ = [], []
    for n, (src, dst) in enumerate(((q_in, qh), (k_in, kh), (v_in, vh))):
        swaps.append(
            remote(src.at[:, :, theirs], dst.at[own_rows], swap_send.at[n], swap_recv.at[n], sibling)
        )
        locals_.append(
            pltpu.make_async_copy(src.at[:, :, mine], dst.at[own_rows], local_sem.at[n])
        )
    for n in range(3):
        swaps[n].start()
        locals_[n].start()

    share = w_in.shape[0]

    def block_rows(way, distance):
        return pl.ds(pl.multiple_of(plane(distance if way else -distance) * share, 16), share)

    def ring_copy(way, distance):
        jump = 2 - distance % 2
        begin = distance - jump
        rows = block_rows(way, begin)
        src = w_in.at[:, mine] if begin == 0 else weight.at[core, rows]
        return remote(
            src, weight.at[core, rows], ring_send.at[way, distance],
            ring_recv.at[way, distance], (plane(-jump if way else jump), me),
        )

    def side_copy(way, distance):
        rows = weight.at[core, block_rows(way, distance)]
        return remote(
            rows, rows, side_send.at[way, distance], side_recv.at[way, distance], sibling
        )

    def ring_start(begin):
        for way in range(2):
            for distance in (begin + 2, begin + 1):
                if distance <= reach[way]:
                    ring_copy(way, distance).start()

    def ring_arrive(distance):
        for way in range(2):
            if distance <= reach[way]:
                ring_copy(way, distance).wait_recv()

    def side_start(distance):
        for way in range(2):
            if distance <= reach[way]:
                side_copy(way, distance).start()

    def ring(begin):
        ring_arrive(begin)
        ring_start(begin)
        side_start(begin)
        ring_arrive(begin - 1)
        side_start(begin - 1)

    ring_start(0)
    weight_own = [
        pltpu.make_async_copy(
            w_in.at[:, pl.ds(half * HALF, HALF)],
            weight.at[half, block_rows(0, 0)], local_sem.at[3 + half],
        )
        for half in range(2)
    ]
    for copy in weight_own:
        copy.start()
    cot_copy = pltpu.make_async_copy(cot_in, cot4, local_sem.at[5])
    cot_copy.start()

    lane = lax.broadcasted_iota(jnp.int32, (1, 128), 1)
    low = jnp.where(lane < HEAD_DIM, 1.0, 0.0).astype(BF16)
    high = jnp.where(lane < HEAD_DIM, 0.0, 1.0).astype(BF16)
    low4 = jnp.concatenate([low] * 4, axis=1)
    high4 = jnp.concatenate([high] * 4, axis=1)
    row_id = lax.broadcasted_iota(jnp.int32, (128, 256), 0)
    col_id = lax.broadcasted_iota(jnp.int32, (128, 256), 1)
    bias[...] = jnp.where(lax.rem(row_id, 2) == lax.rem(col_id, 2), 0.0, -1e30)

    def wide(ref, t):
        return jnp.concatenate([ref[r, :, 128 * t : 128 * t + 128] for r in range(4)], axis=1)

    def terms(left, right, send_ref, t):
        for e, keep in enumerate((low4, high4)):
            h = 2 * t + e
            part = dot(left, right * keep, NT)
            send_ref[8 * (h // 3) : 8 * (h // 3) + 8, h % 3] = part.reshape(8, 16, 128)

    def gathered(ref, h):
        return ref[8 * (h // 3) : 8 * (h // 3) + 8, h % 3].reshape(128, 128)

    def scatter(send_ref, recv_ref, n):
        for to in targets:
            remote(
                send_ref.at[to], recv_ref.at[chip], many_send.at[n], many_recv.at[n],
                (grp, to * 2 + core),
            ).start()
        recv_ref[chip] = send_ref[chip]
        rest = pl.ds(0, CHIPS - 1)
        return remote(
            send_ref.at[rest], recv_ref.at[rest], many_send.at[n], many_recv.at[n], sibling
        )

    def gather(ref, n):
        for to in targets:
            remote(
                ref.at[chip], ref.at[chip], many_send.at[n], many_recv.at[n],
                (grp, to * 2 + core),
            ).start()
        rest = pl.ds(0, CHIPS - 1)
        return remote(ref.at[rest], ref.at[rest], many_send.at[n], many_recv.at[n], sibling)

    def exchange(send_ref, recv_ref, n):
        for partner in targets:
            for to in (partner * 2 + core, partner * 2 + other):
                remote(
                    send_ref.at[to], recv_ref.at[me], many_send.at[n], many_recv.at[n], (grp, to)
                ).start()
        remote(
            send_ref.at[chip * 2 + other], recv_ref.at[me], many_send.at[n], many_recv.at[n],
            sibling,
        ).start()
        recv_ref[me] = send_ref[me]
        rest = pl.ds(0, 2 * CHIPS - 1)
        return remote(
            send_ref.at[rest], recv_ref.at[rest], many_send.at[n], many_recv.at[n], sibling
        )

    sublane = lax.broadcasted_iota(jnp.int32, (16, 8, 128), 1)
    first4 = sublane < 4
    first2 = lax.rem(sublane, 4) < 2

    def swap4(x, y):
        return jnp.where(first4, x, pltpu.roll(y, 4, 1)), jnp.where(first4, pltpu.roll(x, 4, 1), y)

    def swap2(x, y):
        return jnp.where(first2, x, pltpu.roll(y, 2, 1)), jnp.where(first2, pltpu.roll(x, 6, 1), y)

    for n in range(2):
        swaps[n].wait_recv()
        locals_[n].wait()
    for t in range(PAIRS):
        terms(wide(qh, t), wide(kh, t), s_send, t)
    s_all = scatter(s_send, s_recv, 0)
    ring(2)
    s_all.wait_recv()
    scores = jnp.sum(s_recv[...], axis=0) * scale
    shifted = jnp.exp(scores - jnp.max(scores, axis=-1, keepdims=True))
    probs = shifted / jnp.sum(shifted, axis=-1, keepdims=True)
    p_own[...] = probs
    p_all[chip] = probs.astype(BF16)
    p_rest = gather(p_all, 1)
    cot_copy.wait()
    for u in range(6):
        lanes = slice(128 * u, 128 * u + 128)
        g4 = cot4[:, :, lanes].astype(F32)
        for c in range(2):
            cot[c, :, lanes] = g4[:, 2 * c : 2 * c + 2].reshape(128, 128).astype(BF16)
    ring(4)
    swaps[2].wait_recv()
    locals_[2].wait()
    p_rest.wait_recv()

    for t in range(PAIRS):
        values = wide(vh, t)
        z = dot(gathered(p_all, 2 * t), values * low4, NN) + dot(
            gathered(p_all, 2 * t + 1), values * high4, NN
        )
        rows = [z[:, 128 * r : 128 * r + 128].reshape(16, 8, 128) for r in range(4)]
        lanes = slice(128 * t, 128 * t + 128)
        for c, (x, y) in enumerate(zip(swap4(rows[0], rows[2]), swap4(rows[1], rows[3]))):
            block = jnp.concatenate(swap2(x, y), axis=1).astype(BF16)
            for n in range(CHIPS):
                z_send[2 * n + c, :, lanes] = block[n]
    z_rest = exchange(z_send, z_recv, 2)
    for begin in range(6, far + 1, 2):
        ring(begin)

    for copy in weight_own:
        copy.wait()
    for way in range(2):
        for distance in range(1, reach[way] + 1):
            side_copy(way, distance).wait_recv()
    z_rest.wait_recv()

    arrived = z_recv[...].reshape(CHIPS, 2, 16, HALF)
    for half in range(2):
        for t in range(PAIRS):
            z = arrived[:, half, :, 128 * t : 128 * t + 128].astype(F32)
            lanes = slice(half * HALF + 128 * t, half * HALF + 128 * t + 128)
            for c in range(2):
                zh[128 * c : 128 * c + 128, lanes] = (
                    z[:, 8 * c : 8 * c + 8].reshape(128, 128).astype(BF16)
                )
    for part in range(3):
        rows = slice(part * 768, part * 768 + 768)
        w = jnp.concatenate([weight[0, rows], weight[1, rows]], axis=1)
        packed = dot(zh[...], w, NT).astype(BF16)
        for u in range(6):
            abe[6 * part + u] = packed[:, 128 * u : 128 * u + 128]

    @pl.loop(0, 6)
    def _(u):
        lanes = pl.ds(pl.multiple_of(u * 128, 128), 128)
        both = range(2)
        rows = [slice(128 * c, 128 * c + 128) for c in both]
        split = lambda x: jnp.concatenate([x * low, x * high], axis=0)
        stack = lambda x: jnp.concatenate([x[:, :128], x[:, 128:]], axis=0)
        a, b, e = ([abe[6 * n + u, rows[c]] for c in both] for n in range(3))
        g = [cot[c, :, lanes] for c in both]
        a2, b2, e2, g2 = ([split(x) for x in xs] for xs in (a, b, e, g))
        logits = [dot(b[c], a2[c], NT) * 0.125 + bias[...] for c in both]
        slope = [dot(e[c], g2[c], NT) for c in both]
        shifted = [jnp.exp(x - jnp.max(x, axis=0, keepdims=True)) for x in logits]
        weights = [x * (1.0 / jnp.sum(x, axis=0, keepdims=True)) for x in shifted]
        weights_low = [x.astype(BF16) for x in weights]
        mean = [jnp.sum(x * y, axis=0, keepdims=True) for x, y in zip(weights, slope)]
        dlogits = [
            (weights[c] * (slope[c] - mean[c]) * 0.125).astype(BF16) for c in both
        ]
        for c in both:
            att = zh[rows[c], lanes].astype(F32) + dot(stack(weights_low[c]), e2[c], TN)
            outh[c, :, lanes] = att.astype(BF16)
            dabe[12 + u, rows[c]] = dot(weights_low[c], g2[c], NN).astype(BF16)
            dabe[u, rows[c]] = dot(stack(dlogits[c]), b2[c], TN).astype(BF16)
            dabe[6 + u, rows[c]] = dot(dlogits[c], a2[c], NN).astype(BF16)

    dpacked = jnp.concatenate([dabe[n] for n in range(18)], axis=1)
    for half in range(2):
        lanes = slice(half * HALF, half * HALF + HALF)
        back = dot(dpacked, weight[half], NN)
        blocks = jnp.concatenate(
            [
                (cot[c, :, lanes].astype(F32) + back[128 * c : 128 * c + 128]).reshape(16, 8, HALF)
                for c in range(2)
            ],
            axis=1,
        ).astype(BF16)
        for n in range(CHIPS):
            dz_send[2 * n + half] = blocks[n]
    dz_rest = exchange(dz_send, dz_recv, 3)

    for u in range(6):
        lanes = slice(128 * u, 128 * u + 128)
        out4[:, :, lanes] = jnp.concatenate(
            [outh[c, :, lanes].astype(F32).reshape(64, 2, 128) for c in range(2)], axis=1
        ).astype(BF16)
    out_copy = pltpu.make_async_copy(out4, out, local_sem.at[6])
    out_copy.start()
    for copy in swaps:
        copy.wait_send()
    for way in range(2):
        for distance in range(1, reach[way] + 1):
            ring_copy(way, distance).wait_send()
            side_copy(way, distance).wait_send()
    for rest in (s_all, p_rest, z_rest):
        rest.wait_send()
    dz_rest.wait_recv()

    for t in range(PAIRS):
        lanes = slice(128 * t, 128 * t + 128)
        blocks = dz_recv[...].reshape(CHIPS, 2, 16, HALF)[:, :, :, lanes].astype(F32)
        x02, x13 = zip(*[swap2(blocks[:, c, :8], blocks[:, c, 8:]) for c in range(2)])
        r0, r2 = swap4(*x02)
        r1, r3 = swap4(*x13)
        dz = jnp.concatenate(
            [x.reshape(128, 128).astype(BF16) for x in (r0, r1, r2, r3)], axis=1
        )
        dz_rows[t] = dz
        terms(dz, wide(vh, t), g_send, t)
    g_rest = scatter(g_send, g_recv, 4)

    def store(ref, t, x):
        for r in range(4):
            ref[r, :, 128 * t : 128 * t + 128] = x[:, 128 * r : 128 * r + 128].astype(BF16)

    def give_back(ref, out_ref, n):
        local = pltpu.make_async_copy(ref.at[own_rows], out_ref.at[:, :, mine], local_sem.at[7 + n])
        away = remote(
            ref.at[their_rows], out_ref.at[:, :, mine], back_send.at[n], back_recv.at[n], sibling
        )
        landing = remote(
            ref.at[their_rows], out_ref.at[:, :, theirs], back_send.at[n], back_recv.at[n], sibling
        )
        local.start()
        away.start()
        return local, away, landing

    for t in range(PAIRS):
        dz = dz_rows[t]
        store(gvh, t, dot(gathered(p_all, 2 * t), dz * low4, TN)
              + dot(gathered(p_all, 2 * t + 1), dz * high4, TN))
    returned = [give_back(gvh, gv_out, 0)]

    dz_rest.wait_send()
    g_rest.wait_recv()
    slope = jnp.sum(g_recv[...], axis=0)
    probs = p_own[...]
    mean = jnp.sum(probs * slope, axis=-1, keepdims=True)
    ds_all[chip] = (probs * (slope - mean) * scale).astype(BF16)
    ds_rest = gather(ds_all, 5)
    out_copy.wait()
    g_rest.wait_send()
    ds_rest.wait_recv()
    for t in range(PAIRS):
        keys = wide(kh, t)
        store(gqh, t, dot(gathered(ds_all, 2 * t), keys * low4, NN)
              + dot(gathered(ds_all, 2 * t + 1), keys * high4, NN))
    returned.append(give_back(gqh, gq_out, 1))
    for t in range(PAIRS):
        query = wide(qh, t)
        store(gkh, t, dot(gathered(ds_all, 2 * t), query * low4, TN)
              + dot(gathered(ds_all, 2 * t + 1), query * high4, TN))
    returned.append(give_back(gkh, gk_out, 2))

    ds_rest.wait_send()
    for local, away, landing in returned:
        local.wait()
        away.wait_send()
        landing.wait_recv()


def on_device(planes, row_query, row_key, row_value, column_weight, cotangent):
    own_rows, columns, width = row_query.shape
    share = column_weight.shape[1]
    rows, own_columns, _ = cotangent.shape
    vmem = pltpu.VMEM
    sem = pltpu.SemaphoreType.DMA
    row_shape = jax.ShapeDtypeStruct((own_rows, columns, width), BF16)
    shapes = (jax.ShapeDtypeStruct(cotangent.shape, BF16), row_shape, row_shape, row_shape)
    results = pl.pallas_call(
        functools.partial(kernel, planes),
        out_shape=shapes,
        in_specs=[pl.BlockSpec(memory_space=pl.ANY)] * 5,
        out_specs=[pl.BlockSpec(memory_space=pl.ANY)] * 4,
        scratch_shapes=[
            vmem((4, 128, HALF), BF16),
            vmem((4, 128, HALF), BF16),
            vmem((4, 128, HALF), BF16),
            vmem((rows, own_columns, width), BF16),
            vmem((2, 128, 768), BF16),
            vmem((2, planes * share, HALF), BF16),
            vmem((128, 256), F32),
            vmem((CHIPS, 3, 16, 128), F32),
            vmem((CHIPS, 3, 16, 128), F32),
            vmem((3, 16, 128), F32),
            vmem((CHIPS, 3, 16, 128), BF16),
            vmem((2 * CHIPS, 16, HALF), BF16),
            vmem((2 * CHIPS, 16, HALF), BF16),
            vmem((256, 768), BF16),
            vmem((18, 256, 128), BF16),
            vmem((18, 256, 128), BF16),
            vmem((2, 128, 768), BF16),
            vmem((rows, own_columns, width), BF16),
            vmem((2 * CHIPS, 16, HALF), BF16),
            vmem((2 * CHIPS, 16, HALF), BF16),
            vmem((PAIRS, 128, 512), BF16),
            vmem((CHIPS, 3, 16, 128), F32),
            vmem((CHIPS, 3, 16, 128), F32),
            vmem((CHIPS, 3, 16, 128), BF16),
            vmem((4, 128, HALF), BF16),
            vmem((4, 128, HALF), BF16),
            vmem((4, 128, HALF), BF16),
            sem((10,)),
            sem((3,)), sem((3,)),
            sem((2, planes)), sem((2, planes)),
            sem((2, planes)), sem((2, planes)),
            sem((6,)), sem((6,)),
            sem((3,)), sem((3,)),
        ],
        compiler_params=pltpu.CompilerParams(
            collective_id=0, has_side_effects=True, vmem_limit_bytes=VMEM_LIMIT
        ),
    )(row_query, row_key, row_value, column_weight.T, cotangent)
    return pl.pallas_call(
        copy_out,
        out_shape=shapes,
        in_specs=[pl.BlockSpec(memory_space=pl.ANY)] * 4,
        out_specs=[pl.BlockSpec(memory_space=pl.ANY)] * 4,
        scratch_shapes=[vmem(x.shape, BF16) for x in shapes] + [sem((8,)), sem((8,))],
        compiler_params=pltpu.CompilerParams(vmem_limit_bytes=VMEM_LIMIT),
    )(*results)


def solution(mesh):
    planes = mesh.shape["grp"]
    in_specs = (
        P(("grp", "seq"), None, None),
        P(("grp", "seq"), None, None),
        P(("grp", "seq"), None, None),
        P(None, "grp"),
        P("grp", "seq", None),
    )
    out_specs = (
        P("grp", "seq", None),
        P(("grp", "seq"), None, None),
        P(("grp", "seq"), None, None),
        P(("grp", "seq"), None, None),
    )
    return jax.shard_map(
        functools.partial(on_device, planes),
        mesh=mesh, in_specs=in_specs, out_specs=out_specs, check_vma=False,
    )
```

```python
import functools
import math

import jax
import jax.numpy as jnp
from jax import lax
from jax.experimental import pallas as pl
from jax.experimental.pallas import tpu as pltpu
from jax.sharding import PartitionSpec as P

HEADS = 12
HEAD_DIM = 64
CHIPS = 16
SIDE = 4
HALF = 384
PAIRS = 3
MESH = pl.DeviceIdType.MESH
VMEM_LIMIT = 60 * 1024 * 1024
F32 = jnp.float32
BF16 = jnp.bfloat16

NN = (((1,), (0,)), ((), ()))
NT = (((1,), (1,)), ((), ()))
TN = (((0,), (0,)), ((), ()))


def dot(x, y, dims):
    return lax.dot_general(x, y, dims, preferred_element_type=F32)


def copy_out(*refs):
    sources, targets, held, in_sem, out_sem = refs[:4], refs[4:8], refs[8:12], refs[12], refs[13]
    pieces = []
    for n in range(4):
        half = sources[n].shape[0] // 2
        for m in range(2):
            rows = pl.ds(m * half, half)
            pieces.append((
                pltpu.make_async_copy(sources[n].at[rows], held[n].at[rows], in_sem.at[2 * n + m]),
                pltpu.make_async_copy(held[n].at[rows], targets[n].at[rows], out_sem.at[2 * n + m]),
            ))
    for arrive, _ in pieces:
        arrive.start()
    for arrive, leave in pieces:
        arrive.wait()
        leave.start()
    for _, leave in pieces:
        leave.wait()


def kernel(
    planes,
    q_in, k_in, v_in, w_in, cot_in,
    out, gq_out, gk_out, gv_out,
    qh, kh, vh, cot4, cot, weight, bias,
    s_send, s_recv, p_own, p_all, z_send, z_recv, zh, abe, dabe, outh, out4,
    dz_send, dz_recv, dz_rows, g_send, g_recv, ds_all, gqh, gkh, gvh,
    local_sem, swap_send, swap_recv, ring_send, ring_recv, mate_send, mate_recv,
    side_send, side_recv,
    many_send, many_recv, back_send, back_recv,
):
    grp = lax.axis_index("grp")
    me = lax.axis_index("seq")
    chip = lax.div(me, 2)
    core = lax.rem(me, 2)
    other = 1 - core
    chip_x, chip_y = lax.rem(chip, SIDE), lax.div(chip, SIDE)
    sibling = (grp, chip * 2 + other)
    far = planes // 2
    reach = (far, planes - 1 - far)

    def plane(step):
        return lax.rem(grp + planes + step, planes)

    scale = 1.0 / (math.sqrt(HEAD_DIM) * math.sqrt(4 * CHIPS))

    def hops(k):
        return min(k % SIDE, SIDE - k % SIDE) + min(k // SIDE, SIDE - k // SIDE)

    targets = [
        lax.rem(chip_y + k // SIDE, SIDE) * SIDE + lax.rem(chip_x + k % SIDE, SIDE)
        for k in sorted(range(1, CHIPS), key=lambda k: -hops(k))
    ]

    def remote(src, dst, send, recv, device):
        return pltpu.make_async_remote_copy(
            src_ref=src, dst_ref=dst, send_sem=send, recv_sem=recv,
            device_id=device, device_id_type=MESH,
        )

    barrier = pltpu.get_barrier_semaphore()

    @pl.loop(1, 2 * CHIPS)
    def _(k):
        pl.semaphore_signal(
            barrier, inc=1, device_id=(grp, lax.rem(me + k, 2 * CHIPS)), device_id_type=MESH
        )

    near = (-2, -1, 1, 2)
    for step in near:
        pl.semaphore_signal(barrier, inc=1, device_id=(plane(step), me), device_id_type=MESH)
    pl.semaphore_wait(barrier, 2 * CHIPS - 1 + len(near))

    mine = pl.ds(pl.multiple_of(core * HALF, HALF), HALF)
    theirs = pl.ds(pl.multiple_of(other * HALF, HALF), HALF)
    own_rows = pl.ds(core * 2, 2)
    their_rows = pl.ds(other * 2, 2)
    swaps, locals_ = [], []
    for n, (src, dst) in enumerate(((q_in, qh), (k_in, kh), (v_in, vh))):
        swaps.append(
            remote(src.at[:, :, theirs], dst.at[own_rows], swap_send.at[n], swap_recv.at[n], sibling)
        )
        locals_.append(
            pltpu.make_async_copy(src.at[:, :, mine], dst.at[own_rows], local_sem.at[n])
        )
    for n in range(3):
        swaps[n].start()
        locals_[n].start()

    share = w_in.shape[0]
    lead = (share // 16 + 1) // 2 * 16
    tail = share - lead
    parity = (lax.rem(chip_x, 2), lax.rem(chip_y, 2))
    mate = (
        (grp, (chip + 1 - 2 * parity[0]) * 2 + core),
        (grp, (chip + SIDE - 2 * SIDE * parity[1]) * 2 + core),
    )

    def block_begin(way, distance):
        return plane(distance if way else -distance) * share

    def part_rows(way, distance, part):
        begin = (parity[way] * tail, parity[way] * lead, (1 - parity[way]) * lead)[part]
        size = (lead, tail, tail)[part]
        return pl.ds(pl.multiple_of(block_begin(way, distance) + begin, 16), size)

    def ring_copy(way, distance):
        jump = 2 - distance % 2
        begin = distance - jump
        rows = part_rows(way, begin, 0)
        if begin == 0:
            src = w_in.at[pl.ds(pl.multiple_of(parity[way] * tail, 16), lead), mine]
        else:
            src = weight.at[core, rows]
        return remote(
            src, weight.at[core, rows], ring_send.at[way, distance],
            ring_recv.at[way, distance], (plane(-jump if way else jump), me),
        )

    def mate_copy(way, distance):
        rows = weight.at[core, part_rows(way, distance, 1)]
        return remote(rows, rows, mate_send.at[way, distance], mate_recv.at[way, distance], mate[way])

    def mate_landing(way, distance):
        rows = weight.at[core, part_rows(way, distance, 2)]
        return remote(rows, rows, mate_send.at[way, distance], mate_recv.at[way, distance], mate[way])

    def side_copy(way, distance, part):
        rows = weight.at[core, part_rows(way, distance, 2 * part)]
        return remote(
            rows, rows, side_send.at[way, distance, part], side_recv.at[way, distance, part], sibling
        )

    def side_landing(way, distance, part):
        rows = weight.at[other, part_rows(way, distance, 2 * part)]
        return remote(
            rows, rows, side_send.at[way, distance, part], side_recv.at[way, distance, part], sibling
        )

    def ring_start(begin):
        for way in range(2):
            for distance in (begin + 2, begin + 1):
                if distance <= reach[way]:
                    ring_copy(way, distance).start()

    def ring_arrive(distance):
        for way in range(2):
            if distance <= reach[way]:
                ring_copy(way, distance).wait_recv()

    def share_start(distance):
        for way in range(2):
            if distance <= reach[way]:
                mate_copy(way, distance).start()
                side_copy(way, distance, 0).start()

    def ring(begin):
        ring_arrive(begin)
        ring_start(begin)
        share_start(begin)
        ring_arrive(begin - 1)
        share_start(begin - 1)

    def mated(begin):
        for distance in (begin, begin - 1):
            for way in range(2):
                if distance <= reach[way]:
                    mate_landing(way, distance).wait_recv()
                    side_copy(way, distance, 1).start()

    ring_start(0)
    weight_own = [
        pltpu.make_async_copy(
            w_in.at[:, pl.ds(half * HALF, HALF)],
            weight.at[half, pl.ds(pl.multiple_of(block_begin(0, 0), 16), share)], local_sem.at[3 + half],
        )
        for half in range(2)
    ]
    for copy in weight_own:
        copy.start()
    cot_copy = pltpu.make_async_copy(cot_in, cot4, local_sem.at[5])
    cot_copy.start()

    lane = lax.broadcasted_iota(jnp.int32, (1, 128), 1)
    low = jnp.where(lane < HEAD_DIM, 1.0, 0.0).astype(BF16)
    high = jnp.where(lane < HEAD_DIM, 0.0, 1.0).astype(BF16)
    low4 = jnp.concatenate([low] * 4, axis=1)
    high4 = jnp.concatenate([high] * 4, axis=1)
    row_id = lax.broadcasted_iota(jnp.int32, (128, 256), 0)
    col_id = lax.broadcasted_iota(jnp.int32, (128, 256), 1)
    bias[...] = jnp.where(lax.rem(row_id, 2) == lax.rem(col_id, 2), 0.0, -1e30)

    def wide(ref, t):
        return jnp.concatenate([ref[r, :, 128 * t : 128 * t + 128] for r in range(4)], axis=1)

    def terms(left, right, send_ref, t):
        for e, keep in enumerate((low4, high4)):
            h = 2 * t + e
            part = dot(left, right * keep, NT)
            send_ref[8 * (h // 3) : 8 * (h // 3) + 8, h % 3] = part.reshape(8, 16, 128)

    def gathered(ref, h):
        return ref[8 * (h // 3) : 8 * (h // 3) + 8, h % 3].reshape(128, 128)

    def scatter(send_ref, recv_ref, n):
        for to in targets:
            remote(
                send_ref.at[to], recv_ref.at[chip], many_send.at[n], many_recv.at[n],
                (grp, to * 2 + core),
            ).start()
        recv_ref[chip] = send_ref[chip]
        rest = pl.ds(0, CHIPS - 1)
        return remote(
            send_ref.at[rest], recv_ref.at[rest], many_send.at[n], many_recv.at[n], sibling
        )

    def gather(ref, n):
        for to in targets:
            remote(
                ref.at[chip], ref.at[chip], many_send.at[n], many_recv.at[n],
                (grp, to * 2 + core),
            ).start()
        rest = pl.ds(0, CHIPS - 1)
        return remote(ref.at[rest], ref.at[rest], many_send.at[n], many_recv.at[n], sibling)

    def exchange(send_ref, recv_ref, n):
        for partner in targets:
            for to in (partner * 2 + core, partner * 2 + other):
                remote(
                    send_ref.at[to], recv_ref.at[me], many_send.at[n], many_recv.at[n], (grp, to)
                ).start()
        remote(
            send_ref.at[chip * 2 + other], recv_ref.at[me], many_send.at[n], many_recv.at[n],
            sibling,
        ).start()
        recv_ref[me] = send_ref[me]
        rest = pl.ds(0, 2 * CHIPS - 1)
        return remote(
            send_ref.at[rest], recv_ref.at[rest], many_send.at[n], many_recv.at[n], sibling
        )

    sublane = lax.broadcasted_iota(jnp.int32, (16, 8, 128), 1)
    first4 = sublane < 4
    first2 = lax.rem(sublane, 4) < 2

    def swap4(x, y):
        return jnp.where(first4, x, pltpu.roll(y, 4, 1)), jnp.where(first4, pltpu.roll(x, 4, 1), y)

    def swap2(x, y):
        return jnp.where(first2, x, pltpu.roll(y, 2, 1)), jnp.where(first2, pltpu.roll(x, 6, 1), y)

    for n in range(2):
        swaps[n].wait_recv()
        locals_[n].wait()
    for t in range(PAIRS):
        terms(wide(qh, t), wide(kh, t), s_send, t)
    s_all = scatter(s_send, s_recv, 0)
    ring(2)
    s_all.wait_recv()
    scores = jnp.sum(s_recv[...], axis=0) * scale
    shifted = jnp.exp(scores - jnp.max(scores, axis=-1, keepdims=True))
    probs = shifted / jnp.sum(shifted, axis=-1, keepdims=True)
    p_own[...] = probs
    p_all[chip] = probs.astype(BF16)
    p_rest = gather(p_all, 1)
    cot_copy.wait()
    for u in range(6):
        lanes = slice(128 * u, 128 * u + 128)
        g4 = cot4[:, :, lanes].astype(F32)
        for c in range(2):
            cot[c, :, lanes] = g4[:, 2 * c : 2 * c + 2].reshape(128, 128).astype(BF16)
    ring(4)
    mated(2)
    swaps[2].wait_recv()
    locals_[2].wait()
    p_rest.wait_recv()

    for t in range(PAIRS):
        values = wide(vh, t)
        z = dot(gathered(p_all, 2 * t), values * low4, NN) + dot(
            gathered(p_all, 2 * t + 1), values * high4, NN
        )
        rows = [z[:, 128 * r : 128 * r + 128].reshape(16, 8, 128) for r in range(4)]
        lanes = slice(128 * t, 128 * t + 128)
        for c, (x, y) in enumerate(zip(swap4(rows[0], rows[2]), swap4(rows[1], rows[3]))):
            block = jnp.concatenate(swap2(x, y), axis=1).astype(BF16)
            for n in range(CHIPS):
                z_send[2 * n + c, :, lanes] = block[n]
    z_rest = exchange(z_send, z_recv, 2)
    for begin in range(6, far + 1, 2):
        ring(begin)
        mated(begin - 2)
    mated(far)

    for copy in weight_own:
        copy.wait()
    for way in range(2):
        for distance in range(1, reach[way] + 1):
            for part in range(2):
                side_landing(way, distance, part).wait_recv()
    z_rest.wait_recv()

    arrived = z_recv[...].reshape(CHIPS, 2, 16, HALF)
    for half in range(2):
        for t in range(PAIRS):
            z = arrived[:, half, :, 128 * t : 128 * t + 128].astype(F32)
            lanes = slice(half * HALF + 128 * t, half * HALF + 128 * t + 128)
            for c in range(2):
                zh[128 * c : 128 * c + 128, lanes] = (
                    z[:, 8 * c : 8 * c + 8].reshape(128, 128).astype(BF16)
                )
    for part in range(3):
        rows = slice(part * 768, part * 768 + 768)
        w = jnp.concatenate([weight[0, rows], weight[1, rows]], axis=1)
        packed = dot(zh[...], w, NT).astype(BF16)
        for u in range(6):
            abe[6 * part + u] = packed[:, 128 * u : 128 * u + 128]

    @pl.loop(0, 6)
    def _(u):
        lanes = pl.ds(pl.multiple_of(u * 128, 128), 128)
        both = range(2)
        rows = [slice(128 * c, 128 * c + 128) for c in both]
        split = lambda x: jnp.concatenate([x * low, x * high], axis=0)
        stack = lambda x: jnp.concatenate([x[:, :128], x[:, 128:]], axis=0)
        a, b, e = ([abe[6 * n + u, rows[c]] for c in both] for n in range(3))
        g = [cot[c, :, lanes] for c in both]
        a2, b2, e2, g2 = ([split(x) for x in xs] for xs in (a, b, e, g))
        logits = [dot(b[c], a2[c], NT) * 0.125 + bias[...] for c in both]
        slope = [dot(e[c], g2[c], NT) for c in both]
        shifted = [jnp.exp(x - jnp.max(x, axis=0, keepdims=True)) for x in logits]
        weights = [x * (1.0 / jnp.sum(x, axis=0, keepdims=True)) for x in shifted]
        weights_low = [x.astype(BF16) for x in weights]
        mean = [jnp.sum(x * y, axis=0, keepdims=True) for x, y in zip(weights, slope)]
        dlogits = [
            (weights[c] * (slope[c] - mean[c]) * 0.125).astype(BF16) for c in both
        ]
        for c in both:
            att = zh[rows[c], lanes].astype(F32) + dot(stack(weights_low[c]), e2[c], TN)
            outh[c, :, lanes] = att.astype(BF16)
            dabe[12 + u, rows[c]] = dot(weights_low[c], g2[c], NN).astype(BF16)
            dabe[u, rows[c]] = dot(stack(dlogits[c]), b2[c], TN).astype(BF16)
            dabe[6 + u, rows[c]] = dot(dlogits[c], a2[c], NN).astype(BF16)

    dpacked = jnp.concatenate([dabe[n] for n in range(18)], axis=1)
    for half in range(2):
        lanes = slice(half * HALF, half * HALF + HALF)
        back = dot(dpacked, weight[half], NN)
        blocks = jnp.concatenate(
            [
                (cot[c, :, lanes].astype(F32) + back[128 * c : 128 * c + 128]).reshape(16, 8, HALF)
                for c in range(2)
            ],
            axis=1,
        ).astype(BF16)
        for n in range(CHIPS):
            dz_send[2 * n + half] = blocks[n]
    dz_rest = exchange(dz_send, dz_recv, 3)

    for u in range(6):
        lanes = slice(128 * u, 128 * u + 128)
        out4[:, :, lanes] = jnp.concatenate(
            [outh[c, :, lanes].astype(F32).reshape(64, 2, 128) for c in range(2)], axis=1
        ).astype(BF16)
    out_copy = pltpu.make_async_copy(out4, out, local_sem.at[6])
    out_copy.start()
    for copy in swaps:
        copy.wait_send()
    for way in range(2):
        for distance in range(1, reach[way] + 1):
            ring_copy(way, distance).wait_send()
            mate_copy(way, distance).wait_send()
            for part in range(2):
                side_copy(way, distance, part).wait_send()
    for rest in (s_all, p_rest, z_rest):
        rest.wait_send()
    dz_rest.wait_recv()

    for t in range(PAIRS):
        lanes = slice(128 * t, 128 * t + 128)
        blocks = dz_recv[...].reshape(CHIPS, 2, 16, HALF)[:, :, :, lanes].astype(F32)
        x02, x13 = zip(*[swap2(blocks[:, c, :8], blocks[:, c, 8:]) for c in range(2)])
        r0, r2 = swap4(*x02)
        r1, r3 = swap4(*x13)
        dz = jnp.concatenate(
            [x.reshape(128, 128).astype(BF16) for x in (r0, r1, r2, r3)], axis=1
        )
        dz_rows[t] = dz
        terms(dz, wide(vh, t), g_send, t)
    g_rest = scatter(g_send, g_recv, 4)

    def store(ref, t, x):
        for r in range(4):
            ref[r, :, 128 * t : 128 * t + 128] = x[:, 128 * r : 128 * r + 128].astype(BF16)

    def give_back(ref, out_ref, n):
        local = pltpu.make_async_copy(ref.at[own_rows], out_ref.at[:, :, mine], local_sem.at[7 + n])
        away = remote(
            ref.at[their_rows], out_ref.at[:, :, mine], back_send.at[n], back_recv.at[n], sibling
        )
        landing = remote(
            ref.at[their_rows], out_ref.at[:, :, theirs], back_send.at[n], back_recv.at[n], sibling
        )
        local.start()
        away.start()
        return local, away, landing

    for t in range(PAIRS):
        dz = dz_rows[t]
        store(gvh, t, dot(gathered(p_all, 2 * t), dz * low4, TN)
              + dot(gathered(p_all, 2 * t + 1), dz * high4, TN))
    returned = [give_back(gvh, gv_out, 0)]

    dz_rest.wait_send()
    g_rest.wait_recv()
    slope = jnp.sum(g_recv[...], axis=0)
    probs = p_own[...]
    mean = jnp.sum(probs * slope, axis=-1, keepdims=True)
    ds_all[chip] = (probs * (slope - mean) * scale).astype(BF16)
    ds_rest = gather(ds_all, 5)
    out_copy.wait()
    g_rest.wait_send()
    ds_rest.wait_recv()
    for t in range(PAIRS):
        keys = wide(kh, t)
        store(gqh, t, dot(gathered(ds_all, 2 * t), keys * low4, NN)
              + dot(gathered(ds_all, 2 * t + 1), keys * high4, NN))
    returned.append(give_back(gqh, gq_out, 1))
    for t in range(PAIRS):
        query = wide(qh, t)
        store(gkh, t, dot(gathered(ds_all, 2 * t), query * low4, TN)
              + dot(gathered(ds_all, 2 * t + 1), query * high4, TN))
    returned.append(give_back(gkh, gk_out, 2))

    ds_rest.wait_send()
    for local, away, landing in returned:
        local.wait()
        away.wait_send()
        landing.wait_recv()


def on_device(planes, row_query, row_key, row_value, column_weight, cotangent):
    own_rows, columns, width = row_query.shape
    share = column_weight.shape[1]
    rows, own_columns, _ = cotangent.shape
    vmem = pltpu.VMEM
    sem = pltpu.SemaphoreType.DMA
    row_shape = jax.ShapeDtypeStruct((own_rows, columns, width), BF16)
    shapes = (jax.ShapeDtypeStruct(cotangent.shape, BF16), row_shape, row_shape, row_shape)
    results = pl.pallas_call(
        functools.partial(kernel, planes),
        out_shape=shapes,
        in_specs=[pl.BlockSpec(memory_space=pl.ANY)] * 5,
        out_specs=[pl.BlockSpec(memory_space=pl.ANY)] * 4,
        scratch_shapes=[
            vmem((4, 128, HALF), BF16),
            vmem((4, 128, HALF), BF16),
            vmem((4, 128, HALF), BF16),
            vmem((rows, own_columns, width), BF16),
            vmem((2, 128, 768), BF16),
            vmem((2, planes * share, HALF), BF16),
            vmem((128, 256), F32),
            vmem((CHIPS, 3, 16, 128), F32),
            vmem((CHIPS, 3, 16, 128), F32),
            vmem((3, 16, 128), F32),
            vmem((CHIPS, 3, 16, 128), BF16),
            vmem((2 * CHIPS, 16, HALF), BF16),
            vmem((2 * CHIPS, 16, HALF), BF16),
            vmem((256, 768), BF16),
            vmem((18, 256, 128), BF16),
            vmem((18, 256, 128), BF16),
            vmem((2, 128, 768), BF16),
            vmem((rows, own_columns, width), BF16),
            vmem((2 * CHIPS, 16, HALF), BF16),
            vmem((2 * CHIPS, 16, HALF), BF16),
            vmem((PAIRS, 128, 512), BF16),
            vmem((CHIPS, 3, 16, 128), F32),
            vmem((CHIPS, 3, 16, 128), F32),
            vmem((CHIPS, 3, 16, 128), BF16),
            vmem((4, 128, HALF), BF16),
            vmem((4, 128, HALF), BF16),
            vmem((4, 128, HALF), BF16),
            sem((10,)),
            sem((3,)), sem((3,)),
            sem((2, planes)), sem((2, planes)),
            sem((2, planes)), sem((2, planes)),
            sem((2, planes, 2)), sem((2, planes, 2)),
            sem((6,)), sem((6,)),
            sem((3,)), sem((3,)),
        ],
        compiler_params=pltpu.CompilerParams(
            collective_id=0, has_side_effects=True, vmem_limit_bytes=VMEM_LIMIT
        ),
    )(row_query, row_key, row_value, column_weight.T, cotangent)
    return pl.pallas_call(
        copy_out,
        out_shape=shapes,
        in_specs=[pl.BlockSpec(memory_space=pl.ANY)] * 4,
        out_specs=[pl.BlockSpec(memory_space=pl.ANY)] * 4,
        scratch_shapes=[vmem(x.shape, BF16) for x in shapes] + [sem((8,)), sem((8,))],
        compiler_params=pltpu.CompilerParams(vmem_limit_bytes=VMEM_LIMIT),
    )(*results)


def solution(mesh):
    planes = mesh.shape["grp"]
    in_specs = (
        P(("grp", "seq"), None, None),
        P(("grp", "seq"), None, None),
        P(("grp", "seq"), None, None),
        P(None, "grp"),
        P("grp", "seq", None),
    )
    out_specs = (
        P("grp", "seq", None),
        P(("grp", "seq"), None, None),
        P(("grp", "seq"), None, None),
        P(("grp", "seq"), None, None),
    )
    return jax.shard_map(
        functools.partial(on_device, planes),
        mesh=mesh, in_specs=in_specs, out_specs=out_specs, check_vma=False,
    )
```

```python
import functools
import math

import jax
import jax.numpy as jnp
from jax import lax
from jax.experimental import pallas as pl
from jax.experimental.pallas import tpu as pltpu
from jax.sharding import PartitionSpec as P

HEADS = 12
HEAD_DIM = 64
CHIPS = 16
SIDE = 4
HALF = 384
PIECES = 2
PAIRS = 3
MESH = pl.DeviceIdType.MESH
VMEM_LIMIT = 60 * 1024 * 1024
F32 = jnp.float32
BF16 = jnp.bfloat16

NN = (((1,), (0,)), ((), ()))
NT = (((1,), (1,)), ((), ()))
TN = (((0,), (0,)), ((), ()))


def dot(x, y, dims):
    return lax.dot_general(x, y, dims, preferred_element_type=F32)


def copy_out(*refs):
    sources, targets, held, in_sem, out_sem = refs[:4], refs[4:8], refs[8:12], refs[12], refs[13]
    pieces = []
    for n in range(4):
        for m in range(PIECES):
            size = sources[n].shape[0] // 2
            rows, lanes = pl.ds(m % 2 * size, size), pl.ds(0, 768)
            pieces.append((
                pltpu.make_async_copy(sources[n].at[rows, :, lanes], held[n].at[rows, :, lanes], in_sem.at[PIECES * n + m]),
                pltpu.make_async_copy(held[n].at[rows, :, lanes], targets[n].at[rows, :, lanes], out_sem.at[PIECES * n + m]),
            ))
    for arrive, _ in pieces:
        arrive.start()
    for arrive, leave in pieces:
        arrive.wait()
        leave.start()
    for _, leave in pieces:
        leave.wait()


def kernel(
    planes,
    q_in, k_in, v_in, w_in, cot_in,
    out, gq_out, gk_out, gv_out,
    qh, kh, vh, cot4, cot, weight, bias,
    s_send, s_recv, p_own, p_all, z_send, z_recv, zh, abe, dabe, outh, out4,
    dz_send, dz_recv, dz_rows, g_send, g_recv, ds_all, gqh, gkh, gvh,
    local_sem, swap_send, swap_recv, ring_send, ring_recv, mate_send, mate_recv,
    side_send, side_recv,
    many_send, many_recv, back_send, back_recv,
):
    grp = lax.axis_index("grp")
    me = lax.axis_index("seq")
    chip = lax.div(me, 2)
    core = lax.rem(me, 2)
    other = 1 - core
    chip_x, chip_y = lax.rem(chip, SIDE), lax.div(chip, SIDE)
    sibling = (grp, chip * 2 + other)
    far = planes // 2
    reach = (far, planes - 1 - far)

    def plane(step):
        return lax.rem(grp + planes + step, planes)

    scale = 1.0 / (math.sqrt(HEAD_DIM) * math.sqrt(4 * CHIPS))

    def hops(k):
        return min(k % SIDE, SIDE - k % SIDE) + min(k // SIDE, SIDE - k // SIDE)

    targets = [
        lax.rem(chip_y + k // SIDE, SIDE) * SIDE + lax.rem(chip_x + k % SIDE, SIDE)
        for k in sorted(range(1, CHIPS), key=lambda k: -hops(k))
    ]

    def remote(src, dst, send, recv, device):
        return pltpu.make_async_remote_copy(
            src_ref=src, dst_ref=dst, send_sem=send, recv_sem=recv,
            device_id=device, device_id_type=MESH,
        )

    barrier = pltpu.get_barrier_semaphore()
    near = (-2, -1, 1, 2)
    for device in (
        [(plane(step), me) for step in near]
        + [(grp, to * 2 + core) for to in targets]
        + [sibling]
    ):
        pl.semaphore_signal(barrier, inc=1, device_id=device, device_id_type=MESH)

    mine = pl.ds(pl.multiple_of(core * HALF, HALF), HALF)
    theirs = pl.ds(pl.multiple_of(other * HALF, HALF), HALF)
    own_rows = pl.ds(core * 2, 2)
    their_rows = pl.ds(other * 2, 2)
    swaps, locals_ = [], []
    for n, (src, dst) in enumerate(((q_in, qh), (k_in, kh), (v_in, vh))):
        swaps.append(
            remote(src.at[:, :, theirs], dst.at[own_rows], swap_send.at[n], swap_recv.at[n], sibling)
        )
        locals_.append(
            pltpu.make_async_copy(src.at[:, :, mine], dst.at[own_rows], local_sem.at[n])
        )
    for n in range(3):
        locals_[n].start()

    share = w_in.shape[0]
    lead = (share // 16 + 1) // 2 * 16
    tail = share - lead
    parity = (lax.rem(chip_x, 2), lax.rem(chip_y, 2))
    mate = (
        (grp, (chip + 1 - 2 * parity[0]) * 2 + core),
        (grp, (chip + SIDE - 2 * SIDE * parity[1]) * 2 + core),
    )

    def block_begin(way, distance):
        return plane(distance if way else -distance) * share

    def part_rows(way, distance, part):
        begin = (parity[way] * tail, parity[way] * lead, (1 - parity[way]) * lead)[part]
        size = (lead, tail, tail)[part]
        return pl.ds(pl.multiple_of(block_begin(way, distance) + begin, 16), size)

    def ring_copy(way, distance):
        jump = 2 - distance % 2
        begin = distance - jump
        rows = part_rows(way, begin, 0)
        if begin == 0:
            src = w_in.at[pl.ds(pl.multiple_of(parity[way] * tail, 16), lead), mine]
        else:
            src = weight.at[core, rows]
        return remote(
            src, weight.at[core, rows], ring_send.at[way, distance],
            ring_recv.at[way, distance], (plane(-jump if way else jump), me),
        )

    def mate_copy(way, distance):
        rows = weight.at[core, part_rows(way, distance, 1)]
        return remote(rows, rows, mate_send.at[way, distance], mate_recv.at[way, distance], mate[way])

    def mate_landing(way, distance):
        rows = weight.at[core, part_rows(way, distance, 2)]
        return remote(rows, rows, mate_send.at[way, distance], mate_recv.at[way, distance], mate[way])

    def side_copy(way, distance, part):
        rows = weight.at[core, part_rows(way, distance, 2 * part)]
        return remote(
            rows, rows, side_send.at[way, distance, part], side_recv.at[way, distance, part], sibling
        )

    def side_landing(way, distance, part):
        rows = weight.at[other, part_rows(way, distance, 2 * part)]
        return remote(
            rows, rows, side_send.at[way, distance, part], side_recv.at[way, distance, part], sibling
        )

    def ring_start(begin):
        for way in range(2):
            for distance in (begin + 2, begin + 1):
                if distance <= reach[way]:
                    ring_copy(way, distance).start()

    def ring_arrive(distance):
        for way in range(2):
            if distance <= reach[way]:
                ring_copy(way, distance).wait_recv()

    def share_start(distance):
        for way in range(2):
            if distance <= reach[way]:
                mate_copy(way, distance).start()
                side_copy(way, distance, 0).start()

    def ring(begin):
        ring_arrive(begin)
        ring_start(begin)
        share_start(begin)
        ring_arrive(begin - 1)
        share_start(begin - 1)

    def mated(begin):
        for distance in (begin, begin - 1):
            for way in range(2):
                if distance <= reach[way]:
                    mate_landing(way, distance).wait_recv()
                    side_copy(way, distance, 1).start()

    weight_own = [
        pltpu.make_async_copy(
            w_in.at[:, pl.ds(half * HALF, HALF)],
            weight.at[half, pl.ds(pl.multiple_of(block_begin(0, 0), 16), share)], local_sem.at[3 + half],
        )
        for half in range(2)
    ]
    for copy in weight_own:
        copy.start()
    cot_copy = pltpu.make_async_copy(cot_in, cot4, local_sem.at[5])
    cot_copy.start()

    pl.semaphore_wait(barrier, CHIPS + len(near))
    ring_start(0)

    for n in range(2):
        swaps[n].start()

    lane = lax.broadcasted_iota(jnp.int32, (1, 128), 1)
    low = jnp.where(lane < HEAD_DIM, 1.0, 0.0).astype(BF16)
    high = jnp.where(lane < HEAD_DIM, 0.0, 1.0).astype(BF16)
    low4 = jnp.concatenate([low] * 4, axis=1)
    high4 = jnp.concatenate([high] * 4, axis=1)
    row_id = lax.broadcasted_iota(jnp.int32, (128, 256), 0)
    col_id = lax.broadcasted_iota(jnp.int32, (128, 256), 1)
    bias[...] = jnp.where(lax.rem(row_id, 2) == lax.rem(col_id, 2), 0.0, -1e30)

    def wide(ref, t):
        return jnp.concatenate([ref[r, :, 128 * t : 128 * t + 128] for r in range(4)], axis=1)

    def terms(left, right, send_ref, t):
        for e, keep in enumerate((low4, high4)):
            h = 2 * t + e
            part = dot(left, right * keep, NT)
            send_ref[8 * (h // 3) : 8 * (h // 3) + 8, h % 3] = part.reshape(8, 16, 128)

    def gathered(ref, h):
        return ref[8 * (h // 3) : 8 * (h // 3) + 8, h % 3].reshape(128, 128)

    def scatter(send_ref, recv_ref, n):
        for to in targets:
            remote(
                send_ref.at[to], recv_ref.at[chip], many_send.at[n], many_recv.at[n],
                (grp, to * 2 + core),
            ).start()
        recv_ref[chip] = send_ref[chip]
        rest = pl.ds(0, CHIPS - 1)
        return remote(
            send_ref.at[rest], recv_ref.at[rest], many_send.at[n], many_recv.at[n], sibling
        )

    def gather(ref, n):
        for to in targets:
            remote(
                ref.at[chip], ref.at[chip], many_send.at[n], many_recv.at[n],
                (grp, to * 2 + core),
            ).start()
        rest = pl.ds(0, CHIPS - 1)
        return remote(ref.at[rest], ref.at[rest], many_send.at[n], many_recv.at[n], sibling)

    def send_block(send_ref, recv_ref, n, to):
        remote(
            send_ref.at[to], recv_ref.at[me], many_send.at[n], many_recv.at[n], (grp, to)
        ).start()

    def exchange_end(send_ref, recv_ref, n):
        send_block(send_ref, recv_ref, n, chip * 2 + other)
        recv_ref[me] = send_ref[me]
        rest = pl.ds(0, 2 * CHIPS - 1)
        return remote(
            send_ref.at[rest], recv_ref.at[rest], many_send.at[n], many_recv.at[n], sibling
        )

    sublane = lax.broadcasted_iota(jnp.int32, (16, 8, 128), 1)
    first4 = sublane < 4
    first2 = lax.rem(sublane, 4) < 2

    def swap4(x, y):
        return jnp.where(first4, x, pltpu.roll(y, 4, 1)), jnp.where(first4, pltpu.roll(x, 4, 1), y)

    def swap2(x, y):
        return jnp.where(first2, x, pltpu.roll(y, 2, 1)), jnp.where(first2, pltpu.roll(x, 6, 1), y)

    for n in range(2):
        swaps[n].wait_recv()
        locals_[n].wait()
    for t in range(PAIRS):
        terms(wide(qh, t), wide(kh, t), s_send, t)
    s_all = scatter(s_send, s_recv, 0)
    swaps[2].start()
    ring(2)
    s_all.wait_recv()
    scores = jnp.sum(s_recv[...], axis=0) * scale
    shifted = jnp.exp(scores - jnp.max(scores, axis=-1, keepdims=True))
    probs = shifted / jnp.sum(shifted, axis=-1, keepdims=True)
    p_own[...] = probs
    p_all[chip] = probs.astype(BF16)
    p_rest = gather(p_all, 1)
    cot_copy.wait()
    for u in range(6):
        lanes = slice(128 * u, 128 * u + 128)
        g4 = cot4[:, :, lanes].astype(F32)
        for c in range(2):
            cot[c, :, lanes] = g4[:, 2 * c : 2 * c + 2].reshape(128, 128).astype(BF16)
    ring(4)
    mated(2)
    swaps[2].wait_recv()
    locals_[2].wait()
    p_rest.wait_recv()

    for t in range(PAIRS):
        values = wide(vh, t)
        z = dot(gathered(p_all, 2 * t), values * low4, NN) + dot(
            gathered(p_all, 2 * t + 1), values * high4, NN
        )
        rows = [z[:, 128 * r : 128 * r + 128].reshape(16, 8, 128) for r in range(4)]
        lanes = slice(128 * t, 128 * t + 128)
        for c, (x, y) in enumerate(zip(swap4(rows[0], rows[2]), swap4(rows[1], rows[3]))):
            block = jnp.concatenate(swap2(x, y), axis=1).astype(BF16)
            for n in range(CHIPS):
                z_send[2 * n + c, :, lanes] = block[n]
    for to in targets:
        send_block(z_send, z_recv, 2, to * 2 + core)
        send_block(z_send, z_recv, 2, to * 2 + other)
    z_rest = exchange_end(z_send, z_recv, 2)
    for begin in range(6, far + 1, 2):
        ring(begin)
        mated(begin - 2)
    mated(far)

    for copy in weight_own:
        copy.wait()
    for way in range(2):
        for distance in range(1, reach[way] + 1):
            for part in range(2):
                side_landing(way, distance, part).wait_recv()
    z_rest.wait_recv()

    arrived = z_recv[...].reshape(CHIPS, 2, 16, HALF)
    for half in range(2):
        for t in range(PAIRS):
            z = arrived[:, half, :, 128 * t : 128 * t + 128].astype(F32)
            lanes = slice(half * HALF + 128 * t, half * HALF + 128 * t + 128)
            for c in range(2):
                zh[128 * c : 128 * c + 128, lanes] = (
                    z[:, 8 * c : 8 * c + 8].reshape(128, 128).astype(BF16)
                )
    for part in range(3):
        rows = slice(part * 768, part * 768 + 768)
        w = jnp.concatenate([weight[0, rows], weight[1, rows]], axis=1)
        packed = dot(zh[...], w, NT).astype(BF16)
        for u in range(6):
            abe[6 * part + u] = packed[:, 128 * u : 128 * u + 128]

    @pl.loop(0, 6, unroll=6)
    def _(u):
        lanes = pl.ds(pl.multiple_of(u * 128, 128), 128)
        both = range(2)
        rows = [slice(128 * c, 128 * c + 128) for c in both]
        split = lambda x: jnp.concatenate([x * low, x * high], axis=0)
        stack = lambda x: jnp.concatenate([x[:, :128], x[:, 128:]], axis=0)
        a, b, e = ([abe[6 * n + u, rows[c]] for c in both] for n in range(3))
        g = [cot[c, :, lanes] for c in both]
        a2, b2, e2, g2 = ([split(x) for x in xs] for xs in (a, b, e, g))
        logits = [dot(b[c], a2[c], NT) * 0.125 + bias[...] for c in both]
        slope = [dot(e[c], g2[c], NT) for c in both]
        shifted = [jnp.exp(x - jnp.max(x, axis=0, keepdims=True)) for x in logits]
        weights = [x * (1.0 / jnp.sum(x, axis=0, keepdims=True)) for x in shifted]
        weights_low = [x.astype(BF16) for x in weights]
        mean = [jnp.sum(x * y, axis=0, keepdims=True) for x, y in zip(weights, slope)]
        dlogits = [
            (weights[c] * (slope[c] - mean[c]) * 0.125).astype(BF16) for c in both
        ]
        for c in both:
            att = zh[rows[c], lanes].astype(F32) + dot(stack(weights_low[c]), e2[c], TN)
            outh[c, :, lanes] = att.astype(BF16)
            dabe[12 + u, rows[c]] = dot(weights_low[c], g2[c], NN).astype(BF16)
            dabe[u, rows[c]] = dot(stack(dlogits[c]), b2[c], TN).astype(BF16)
            dabe[6 + u, rows[c]] = dot(dlogits[c], a2[c], NN).astype(BF16)

    dpacked = jnp.concatenate([dabe[n] for n in range(18)], axis=1)
    for half in range(2):
        lanes = slice(half * HALF, half * HALF + HALF)
        back = dot(dpacked, weight[half], NN)
        blocks = jnp.concatenate(
            [
                (cot[c, :, lanes].astype(F32) + back[128 * c : 128 * c + 128]).reshape(16, 8, HALF)
                for c in range(2)
            ],
            axis=1,
        ).astype(BF16)
        for n in range(CHIPS):
            dz_send[2 * n + half] = blocks[n]
        for to in targets:
            send_block(dz_send, dz_recv, 3, to * 2 + half)
    dz_rest = exchange_end(dz_send, dz_recv, 3)

    for u in range(6):
        lanes = slice(128 * u, 128 * u + 128)
        out4[:, :, lanes] = jnp.concatenate(
            [outh[c, :, lanes].astype(F32).reshape(64, 2, 128) for c in range(2)], axis=1
        ).astype(BF16)
    out_copy = pltpu.make_async_copy(out4, out, local_sem.at[6])
    out_copy.start()
    for copy in swaps:
        copy.wait_send()
    for way in range(2):
        for distance in range(1, reach[way] + 1):
            ring_copy(way, distance).wait_send()
            mate_copy(way, distance).wait_send()
            for part in range(2):
                side_copy(way, distance, part).wait_send()
    for rest in (s_all, p_rest, z_rest):
        rest.wait_send()
    dz_rest.wait_recv()

    for t in range(PAIRS):
        lanes = slice(128 * t, 128 * t + 128)
        blocks = dz_recv[...].reshape(CHIPS, 2, 16, HALF)[:, :, :, lanes].astype(F32)
        x02, x13 = zip(*[swap2(blocks[:, c, :8], blocks[:, c, 8:]) for c in range(2)])
        r0, r2 = swap4(*x02)
        r1, r3 = swap4(*x13)
        dz = jnp.concatenate(
            [x.reshape(128, 128).astype(BF16) for x in (r0, r1, r2, r3)], axis=1
        )
        dz_rows[t] = dz
        terms(dz, wide(vh, t), g_send, t)
    g_rest = scatter(g_send, g_recv, 4)

    def store(ref, t, x):
        for r in range(4):
            ref[r, :, 128 * t : 128 * t + 128] = x[:, 128 * r : 128 * r + 128].astype(BF16)

    def give_back(ref, out_ref, n):
        local = pltpu.make_async_copy(ref.at[own_rows], out_ref.at[:, :, mine], local_sem.at[7 + n])
        away = remote(
            ref.at[their_rows], out_ref.at[:, :, mine], back_send.at[n], back_recv.at[n], sibling
        )
        landing = remote(
            ref.at[their_rows], out_ref.at[:, :, theirs], back_send.at[n], back_recv.at[n], sibling
        )
        local.start()
        away.start()
        return local, away, landing

    for t in range(PAIRS):
        dz = dz_rows[t]
        store(gvh, t, dot(gathered(p_all, 2 * t), dz * low4, TN)
              + dot(gathered(p_all, 2 * t + 1), dz * high4, TN))
    returned = [give_back(gvh, gv_out, 0)]

    dz_rest.wait_send()
    g_rest.wait_recv()
    slope = jnp.sum(g_recv[...], axis=0)
    probs = p_own[...]
    mean = jnp.sum(probs * slope, axis=-1, keepdims=True)
    ds_all[chip] = (probs * (slope - mean) * scale).astype(BF16)
    ds_rest = gather(ds_all, 5)
    out_copy.wait()
    g_rest.wait_send()
    ds_rest.wait_recv()
    for t in range(PAIRS):
        keys = wide(kh, t)
        store(gqh, t, dot(gathered(ds_all, 2 * t), keys * low4, NN)
              + dot(gathered(ds_all, 2 * t + 1), keys * high4, NN))
    returned.append(give_back(gqh, gq_out, 1))
    for t in range(PAIRS):
        query = wide(qh, t)
        store(gkh, t, dot(gathered(ds_all, 2 * t), query * low4, TN)
              + dot(gathered(ds_all, 2 * t + 1), query * high4, TN))
    returned.append(give_back(gkh, gk_out, 2))

    ds_rest.wait_send()
    for local, away, landing in returned:
        local.wait()
        away.wait_send()
        landing.wait_recv()


def on_device(planes, row_query, row_key, row_value, column_weight, cotangent):
    own_rows, columns, width = row_query.shape
    share = column_weight.shape[1]
    rows, own_columns, _ = cotangent.shape
    vmem = pltpu.VMEM
    sem = pltpu.SemaphoreType.DMA
    row_shape = jax.ShapeDtypeStruct((own_rows, columns, width), BF16)
    shapes = (jax.ShapeDtypeStruct(cotangent.shape, BF16), row_shape, row_shape, row_shape)
    results = pl.pallas_call(
        functools.partial(kernel, planes),
        out_shape=shapes,
        in_specs=[pl.BlockSpec(memory_space=pl.ANY)] * 5,
        out_specs=[pl.BlockSpec(memory_space=pl.ANY)] * 4,
        scratch_shapes=[
            vmem((4, 128, HALF), BF16),
            vmem((4, 128, HALF), BF16),
            vmem((4, 128, HALF), BF16),
            vmem((rows, own_columns, width), BF16),
            vmem((2, 128, 768), BF16),
            vmem((2, planes * share, HALF), BF16),
            vmem((128, 256), F32),
            vmem((CHIPS, 3, 16, 128), F32),
            vmem((CHIPS, 3, 16, 128), F32),
            vmem((3, 16, 128), F32),
            vmem((CHIPS, 3, 16, 128), BF16),
            vmem((2 * CHIPS, 16, HALF), BF16),
            vmem((2 * CHIPS, 16, HALF), BF16),
            vmem((256, 768), BF16),
            vmem((18, 256, 128), BF16),
            vmem((18, 256, 128), BF16),
            vmem((2, 128, 768), BF16),
            vmem((rows, own_columns, width), BF16),
            vmem((2 * CHIPS, 16, HALF), BF16),
            vmem((2 * CHIPS, 16, HALF), BF16),
            vmem((PAIRS, 128, 512), BF16),
            vmem((CHIPS, 3, 16, 128), F32),
            vmem((CHIPS, 3, 16, 128), F32),
            vmem((CHIPS, 3, 16, 128), BF16),
            vmem((4, 128, HALF), BF16),
            vmem((4, 128, HALF), BF16),
            vmem((4, 128, HALF), BF16),
            sem((10,)),
            sem((3,)), sem((3,)),
            sem((2, planes)), sem((2, planes)),
            sem((2, planes)), sem((2, planes)),
            sem((2, planes, 2)), sem((2, planes, 2)),
            sem((6,)), sem((6,)),
            sem((3,)), sem((3,)),
        ],
        compiler_params=pltpu.CompilerParams(
            collective_id=0, has_side_effects=True, vmem_limit_bytes=VMEM_LIMIT
        ),
    )(row_query, row_key, row_value, column_weight.T, cotangent)
    return pl.pallas_call(
        copy_out,
        out_shape=shapes,
        in_specs=[pl.BlockSpec(memory_space=pl.ANY)] * 4,
        out_specs=[pl.BlockSpec(memory_space=pl.ANY)] * 4,
        scratch_shapes=[vmem(x.shape, BF16) for x in shapes] + [sem((4 * PIECES,))] * 2,
        compiler_params=pltpu.CompilerParams(vmem_limit_bytes=VMEM_LIMIT),
    )(*results)


def solution(mesh):
    planes = mesh.shape["grp"]
    in_specs = (
        P(("grp", "seq"), None, None),
        P(("grp", "seq"), None, None),
        P(("grp", "seq"), None, None),
        P(None, "grp"),
        P("grp", "seq", None),
    )
    out_specs = (
        P("grp", "seq", None),
        P(("grp", "seq"), None, None),
        P(("grp", "seq"), None, None),
        P(("grp", "seq"), None, None),
    )
    return jax.shard_map(
        functools.partial(on_device, planes),
        mesh=mesh, in_specs=in_specs, out_specs=out_specs, check_vma=False,
    )
```

```python
import functools
import math

import jax
import jax.numpy as jnp
from jax import lax
from jax.experimental import pallas as pl
from jax.experimental.pallas import tpu as pltpu
from jax.sharding import PartitionSpec as P

HEADS = 12
HEAD_DIM = 64
CHIPS = 16
SIDE = 4
HALF = 384
PAIRS = 3
MESH = pl.DeviceIdType.MESH
VMEM_LIMIT = 60 * 1024 * 1024
F32 = jnp.float32
BF16 = jnp.bfloat16

NN = (((1,), (0,)), ((), ()))
NT = (((1,), (1,)), ((), ()))
TN = (((0,), (0,)), ((), ()))


def dot(x, y, dims):
    return lax.dot_general(x, y, dims, preferred_element_type=F32)


def finish(
    q_in, k_in, ds_in, out_in, gv_in,
    out, gq_out, gk_out, gv_out,
    q, k, ds, out_held, gv_held, gq, gk, in_sem, out_sem,
):
    low, high = head_masks(2)
    arrive = [
        pltpu.make_async_copy(src, dst, in_sem.at[n])
        for n, (src, dst) in enumerate(
            ((ds_in, ds), (k_in, k), (q_in, q), (out_in, out_held), (gv_in, gv_held))
        )
    ]
    for copy in arrive:
        copy.start()
    leave = [
        pltpu.make_async_copy(out_held, out, out_sem.at[0]),
        pltpu.make_async_copy(gv_held, gv_out, out_sem.at[1]),
    ]

    def gradient(held, other, dims, target, n):
        for t in range(2 * PAIRS):
            lanes = slice(128 * t, 128 * t + 128)
            x = jnp.concatenate([other[r, :, lanes] for r in range(2)], axis=1)
            total = None
            for e, keep in enumerate((low, high)):
                h = 2 * t + e
                group, place = h % 6 // 3, h % 3
                rows = jnp.concatenate(
                    [ds[h // 6, 8 * group + b, place] for b in range(8)], axis=0
                )
                part = dot(rows, x * keep, dims)
                total = part if total is None else total + part
            for r in range(2):
                held[r, :, lanes] = total[:, 128 * r : 128 * r + 128].astype(BF16)
            if t % PAIRS == PAIRS - 1:
                half = pl.ds(t // PAIRS * HALF, HALF)
                leave.append(
                    pltpu.make_async_copy(
                        held.at[:, :, half], target.at[:, :, half], out_sem.at[n + t // PAIRS]
                    )
                )
                leave[-1].start()

    arrive[0].wait()
    arrive[1].wait()
    gradient(gq, k, NN, gq_out, 2)
    for n in range(2):
        arrive[3 + n].wait()
        leave[n].start()
    arrive[2].wait()
    gradient(gk, q, TN, gk_out, 4)
    for copy in leave:
        copy.wait()


def head_masks(copies):
    lane = lax.broadcasted_iota(jnp.int32, (1, 128), 1)
    low = jnp.where(lane < HEAD_DIM, 1.0, 0.0).astype(BF16)
    high = jnp.where(lane < HEAD_DIM, 0.0, 1.0).astype(BF16)
    return [jnp.concatenate([x] * copies, axis=1) for x in (low, high)]


def kernel(
    planes,
    q_in, k_in, v_in, w_in, cot_in,
    out, ds_out, gv_out,
    qh, kh, vh, cot4, cot, weight, bias,
    s_send, s_recv, p_own, p_all, z_send, z_recv, zh, abe, dabe, outh, out4,
    dz_send, dz_recv, dz_rows, g_send, g_recv, ds_all, gvh,
    local_sem, swap_send, swap_recv, ring_send, ring_recv, mate_send, mate_recv,
    side_send, side_recv,
    many_send, many_recv, back_send, back_recv, row_sem,
):
    grp = lax.axis_index("grp")
    me = lax.axis_index("seq")
    chip = lax.div(me, 2)
    core = lax.rem(me, 2)
    other = 1 - core
    chip_x, chip_y = lax.rem(chip, SIDE), lax.div(chip, SIDE)
    sibling = (grp, chip * 2 + other)
    far = planes // 2
    reach = (far, planes - 1 - far)

    def plane(step):
        return lax.rem(grp + planes + step, planes)

    scale = 1.0 / (math.sqrt(HEAD_DIM) * math.sqrt(4 * CHIPS))

    def hops(k):
        return min(k % SIDE, SIDE - k % SIDE) + min(k // SIDE, SIDE - k // SIDE)

    targets = [
        lax.rem(chip_y + k // SIDE, SIDE) * SIDE + lax.rem(chip_x + k % SIDE, SIDE)
        for k in sorted(range(1, CHIPS), key=lambda k: -hops(k))
    ]

    def remote(src, dst, send, recv, device):
        return pltpu.make_async_remote_copy(
            src_ref=src, dst_ref=dst, send_sem=send, recv_sem=recv,
            device_id=device, device_id_type=MESH,
        )

    barrier = pltpu.get_barrier_semaphore()
    near = (-2, 2, -1, 1)
    column = [(grp, (lax.rem(chip_y + n, SIDE) * SIDE + chip_x) * 2 + core) for n in (2, 1, 3)]
    row = [(grp, (chip_y * SIDE + lax.rem(chip_x + n, SIDE)) * 2 + core) for n in (2, 1, 3)]
    greeted = row + column + [(plane(step), me) for step in near] + [sibling]
    for device in greeted:
        pl.semaphore_signal(barrier, inc=1, device_id=device, device_id_type=MESH)

    mine = pl.ds(pl.multiple_of(core * HALF, HALF), HALF)
    theirs = pl.ds(pl.multiple_of(other * HALF, HALF), HALF)
    own_rows = pl.ds(core * 2, 2)
    their_rows = pl.ds(other * 2, 2)
    swaps, locals_ = [], []
    for n, (src, dst) in enumerate(((q_in, qh), (k_in, kh), (v_in, vh))):
        swaps.append(
            remote(src.at[:, :, theirs], dst.at[own_rows], swap_send.at[n], swap_recv.at[n], sibling)
        )
        locals_.append(
            pltpu.make_async_copy(src.at[:, :, mine], dst.at[own_rows], local_sem.at[n])
        )
    for n in range(3):
        locals_[n].start()

    share = w_in.shape[0]
    lead = (share // 16 + 1) // 2 * 16
    tail = share - lead
    parity = (lax.rem(chip_x, 2), lax.rem(chip_y, 2))
    mate = (
        (grp, (chip + 1 - 2 * parity[0]) * 2 + core),
        (grp, (chip + SIDE - 2 * SIDE * parity[1]) * 2 + core),
    )

    def block_begin(way, distance):
        return plane(distance if way else -distance) * share

    def part_rows(way, distance, part):
        begin = (parity[way] * tail, parity[way] * lead, (1 - parity[way]) * lead)[part]
        size = (lead, tail, tail)[part]
        return pl.ds(pl.multiple_of(block_begin(way, distance) + begin, 16), size)

    def ring_copy(way, distance):
        jump = 2 - distance % 2
        begin = distance - jump
        rows = part_rows(way, begin, 0)
        if begin == 0:
            src = w_in.at[pl.ds(pl.multiple_of(parity[way] * tail, 16), lead), mine]
        else:
            src = weight.at[core, rows]
        return remote(
            src, weight.at[core, rows], ring_send.at[way, distance],
            ring_recv.at[way, distance], (plane(-jump if way else jump), me),
        )

    def mate_copy(way, distance):
        rows = weight.at[core, part_rows(way, distance, 1)]
        return remote(rows, rows, mate_send.at[way, distance], mate_recv.at[way, distance], mate[way])

    def mate_landing(way, distance):
        rows = weight.at[core, part_rows(way, distance, 2)]
        return remote(rows, rows, mate_send.at[way, distance], mate_recv.at[way, distance], mate[way])

    def side_copy(way, distance, part):
        rows = weight.at[core, part_rows(way, distance, 2 * part)]
        return remote(
            rows, rows, side_send.at[way, distance, part], side_recv.at[way, distance, part], sibling
        )

    def side_landing(way, distance, part):
        rows = weight.at[other, part_rows(way, distance, 2 * part)]
        return remote(
            rows, rows, side_send.at[way, distance, part], side_recv.at[way, distance, part], sibling
        )

    def ring_start(begin):
        for way in range(2):
            for distance in (begin + 2, begin + 1):
                if distance <= reach[way]:
                    ring_copy(way, distance).start()

    def ring_arrive(distance):
        for way in range(2):
            if distance <= reach[way]:
                ring_copy(way, distance).wait_recv()

    def share_start(distance):
        for way in range(2):
            if distance <= reach[way]:
                mate_copy(way, distance).start()
                side_copy(way, distance, 0).start()

    def ring(begin):
        ring_arrive(begin)
        ring_start(begin)
        share_start(begin)
        ring_arrive(begin - 1)
        share_start(begin - 1)

    def mated(begin):
        for distance in (begin, begin - 1):
            for way in range(2):
                if distance <= reach[way]:
                    mate_landing(way, distance).wait_recv()
                    side_copy(way, distance, 1).start()

    weight_own = [
        pltpu.make_async_copy(
            w_in.at[:, pl.ds(half * HALF, HALF)],
            weight.at[half, pl.ds(pl.multiple_of(block_begin(0, 0), 16), share)], local_sem.at[3 + half],
        )
        for half in range(2)
    ]
    for copy in weight_own:
        copy.start()
    cot_copy = pltpu.make_async_copy(cot_in, cot4, local_sem.at[5])
    cot_copy.start()

    pl.semaphore_wait(barrier, len(greeted))
    for device in column:
        pl.semaphore_signal(row_sem, inc=1, device_id=device, device_id_type=MESH)
    ring_start(0)

    for n in range(2):
        swaps[n].start()

    low, high = head_masks(1)
    low4, high4 = head_masks(4)
    row_id = lax.broadcasted_iota(jnp.int32, (128, 256), 0)
    col_id = lax.broadcasted_iota(jnp.int32, (128, 256), 1)
    bias[...] = jnp.where(lax.rem(row_id, 2) == lax.rem(col_id, 2), 0.0, -1e30)

    def wide(ref, t):
        return jnp.concatenate([ref[r, :, 128 * t : 128 * t + 128] for r in range(4)], axis=1)

    def terms(left, right, send_ref, t):
        for e, keep in enumerate((low4, high4)):
            h = 2 * t + e
            part = dot(left, right * keep, NT)
            send_ref[8 * (h // 3) : 8 * (h // 3) + 8, h % 3] = part.reshape(8, 16, 128)

    def gathered(ref, h):
        return ref[8 * (h // 3) : 8 * (h // 3) + 8, h % 3].reshape(128, 128)

    def scatter(send_ref, recv_ref, n):
        for to in targets:
            remote(
                send_ref.at[to], recv_ref.at[chip], many_send.at[n], many_recv.at[n],
                (grp, to * 2 + core),
            ).start()
        recv_ref[chip] = send_ref[chip]
        rest = pl.ds(0, CHIPS - 1)
        return remote(
            send_ref.at[rest], recv_ref.at[rest], many_send.at[n], many_recv.at[n], sibling
        )

    def gather(ref, n):
        for to in targets:
            remote(
                ref.at[chip], ref.at[chip], many_send.at[n], many_recv.at[n],
                (grp, to * 2 + core),
            ).start()
        rest = pl.ds(0, CHIPS - 1)
        return remote(ref.at[rest], ref.at[rest], many_send.at[n], many_recv.at[n], sibling)

    def send_block(send_ref, recv_ref, n, to):
        remote(
            send_ref.at[to], recv_ref.at[me], many_send.at[n], many_recv.at[n], (grp, to)
        ).start()

    def exchange_end(send_ref, recv_ref, n):
        send_block(send_ref, recv_ref, n, chip * 2 + other)
        recv_ref[me] = send_ref[me]
        rest = pl.ds(0, 2 * CHIPS - 1)
        return remote(
            send_ref.at[rest], recv_ref.at[rest], many_send.at[n], many_recv.at[n], sibling
        )

    sublane = lax.broadcasted_iota(jnp.int32, (16, 8, 128), 1)
    first4 = sublane < 4
    first2 = lax.rem(sublane, 4) < 2

    def swap4(x, y):
        return jnp.where(first4, x, pltpu.roll(y, 4, 1)), jnp.where(first4, pltpu.roll(x, 4, 1), y)

    def swap2(x, y):
        return jnp.where(first2, x, pltpu.roll(y, 2, 1)), jnp.where(first2, pltpu.roll(x, 6, 1), y)

    for n in range(2):
        swaps[n].wait_recv()
        locals_[n].wait()
    for t in range(PAIRS):
        terms(wide(qh, t), wide(kh, t), s_send, t)
    pl.semaphore_wait(row_sem, len(column))
    s_all = scatter(s_send, s_recv, 0)
    swaps[2].start()
    ring(2)
    s_all.wait_recv()
    scores = jnp.sum(s_recv[...], axis=0) * scale
    shifted = jnp.exp(scores - jnp.max(scores, axis=-1, keepdims=True))
    probs = shifted / jnp.sum(shifted, axis=-1, keepdims=True)
    p_own[...] = probs
    p_all[chip] = probs.astype(BF16)
    p_rest = gather(p_all, 1)
    cot_copy.wait()
    for u in range(6):
        lanes = slice(128 * u, 128 * u + 128)
        g4 = cot4[:, :, lanes].astype(F32)
        for c in range(2):
            cot[c, :, lanes] = g4[:, 2 * c : 2 * c + 2].reshape(128, 128).astype(BF16)
    ring(4)
    mated(2)
    swaps[2].wait_recv()
    locals_[2].wait()
    p_rest.wait_recv()

    for t in range(PAIRS):
        values = wide(vh, t)
        z = dot(gathered(p_all, 2 * t), values * low4, NN) + dot(
            gathered(p_all, 2 * t + 1), values * high4, NN
        )
        rows = [z[:, 128 * r : 128 * r + 128].reshape(16, 8, 128) for r in range(4)]
        lanes = slice(128 * t, 128 * t + 128)
        for c, (x, y) in enumerate(zip(swap4(rows[0], rows[2]), swap4(rows[1], rows[3]))):
            block = jnp.concatenate(swap2(x, y), axis=1).astype(BF16)
            for n in range(CHIPS):
                z_send[2 * n + c, :, lanes] = block[n]
    for to in targets:
        send_block(z_send, z_recv, 2, to * 2 + core)
        send_block(z_send, z_recv, 2, to * 2 + other)
    z_rest = exchange_end(z_send, z_recv, 2)
    for begin in range(6, far + 1, 2):
        ring(begin)
        mated(begin - 2)
    mated(far)

    for copy in weight_own:
        copy.wait()
    for way in range(2):
        for distance in range(1, reach[way] + 1):
            for part in range(2):
                side_landing(way, distance, part).wait_recv()
    z_rest.wait_recv()

    arrived = z_recv[...].reshape(CHIPS, 2, 16, HALF)
    for half in range(2):
        for t in range(PAIRS):
            z = arrived[:, half, :, 128 * t : 128 * t + 128].astype(F32)
            lanes = slice(half * HALF + 128 * t, half * HALF + 128 * t + 128)
            for c in range(2):
                zh[128 * c : 128 * c + 128, lanes] = (
                    z[:, 8 * c : 8 * c + 8].reshape(128, 128).astype(BF16)
                )
    for part in range(3):
        rows = slice(part * 768, part * 768 + 768)
        w = jnp.concatenate([weight[0, rows], weight[1, rows]], axis=1)
        packed = dot(zh[...], w, NT).astype(BF16)
        for u in range(6):
            abe[6 * part + u] = packed[:, 128 * u : 128 * u + 128]

    @pl.loop(0, 6, unroll=6)
    def _(u):
        lanes = pl.ds(pl.multiple_of(u * 128, 128), 128)
        both = range(2)
        rows = [slice(128 * c, 128 * c + 128) for c in both]
        split = lambda x: jnp.concatenate([x * low, x * high], axis=0)
        stack = lambda x: jnp.concatenate([x[:, :128], x[:, 128:]], axis=0)
        a, b, e = ([abe[6 * n + u, rows[c]] for c in both] for n in range(3))
        g = [cot[c, :, lanes] for c in both]
        a2, b2, e2, g2 = ([split(x) for x in xs] for xs in (a, b, e, g))
        logits = [dot(b[c], a2[c], NT) * 0.125 + bias[...] for c in both]
        slope = [dot(e[c], g2[c], NT) for c in both]
        shifted = [jnp.exp(x - jnp.max(x, axis=0, keepdims=True)) for x in logits]
        weights = [x * (1.0 / jnp.sum(x, axis=0, keepdims=True)) for x in shifted]
        weights_low = [x.astype(BF16) for x in weights]
        mean = [jnp.sum(x * y, axis=0, keepdims=True) for x, y in zip(weights, slope)]
        dlogits = [
            (weights[c] * (slope[c] - mean[c]) * 0.125).astype(BF16) for c in both
        ]
        for c in both:
            att = zh[rows[c], lanes].astype(F32) + dot(stack(weights_low[c]), e2[c], TN)
            outh[c, :, lanes] = att.astype(BF16)
            dabe[12 + u, rows[c]] = dot(weights_low[c], g2[c], NN).astype(BF16)
            dabe[u, rows[c]] = dot(stack(dlogits[c]), b2[c], TN).astype(BF16)
            dabe[6 + u, rows[c]] = dot(dlogits[c], a2[c], NN).astype(BF16)

    dpacked = jnp.concatenate([dabe[n] for n in range(18)], axis=1)
    for half in range(2):
        lanes = slice(half * HALF, half * HALF + HALF)
        back = dot(dpacked, weight[half], NN)
        blocks = jnp.concatenate(
            [
                (cot[c, :, lanes].astype(F32) + back[128 * c : 128 * c + 128]).reshape(16, 8, HALF)
                for c in range(2)
            ],
            axis=1,
        ).astype(BF16)
        for n in range(CHIPS):
            dz_send[2 * n + half] = blocks[n]
        for to in targets:
            send_block(dz_send, dz_recv, 3, to * 2 + half)
    dz_rest = exchange_end(dz_send, dz_recv, 3)

    for u in range(6):
        lanes = slice(128 * u, 128 * u + 128)
        out4[:, :, lanes] = jnp.concatenate(
            [outh[c, :, lanes].astype(F32).reshape(64, 2, 128) for c in range(2)], axis=1
        ).astype(BF16)
    out_copy = pltpu.make_async_copy(out4, out, local_sem.at[6])
    out_copy.start()
    for copy in swaps:
        copy.wait_send()
    for way in range(2):
        for distance in range(1, reach[way] + 1):
            ring_copy(way, distance).wait_send()
            mate_copy(way, distance).wait_send()
            for part in range(2):
                side_copy(way, distance, part).wait_send()
    for rest in (s_all, p_rest, z_rest):
        rest.wait_send()
    dz_rest.wait_recv()

    for t in range(PAIRS):
        lanes = slice(128 * t, 128 * t + 128)
        blocks = dz_recv[...].reshape(CHIPS, 2, 16, HALF)[:, :, :, lanes].astype(F32)
        x02, x13 = zip(*[swap2(blocks[:, c, :8], blocks[:, c, 8:]) for c in range(2)])
        r0, r2 = swap4(*x02)
        r1, r3 = swap4(*x13)
        dz = jnp.concatenate(
            [x.reshape(128, 128).astype(BF16) for x in (r0, r1, r2, r3)], axis=1
        )
        dz_rows[t] = dz
        terms(dz, wide(vh, t), g_send, t)
    g_rest = scatter(g_send, g_recv, 4)

    def store(ref, t, x):
        for r in range(4):
            ref[r, :, 128 * t : 128 * t + 128] = x[:, 128 * r : 128 * r + 128].astype(BF16)

    def give_back(ref, out_ref, n):
        local = pltpu.make_async_copy(ref.at[own_rows], out_ref.at[:, :, mine], local_sem.at[7 + n])
        away = remote(
            ref.at[their_rows], out_ref.at[:, :, mine], back_send.at[n], back_recv.at[n], sibling
        )
        landing = remote(
            ref.at[their_rows], out_ref.at[:, :, theirs], back_send.at[n], back_recv.at[n], sibling
        )
        local.start()
        away.start()
        return local, away, landing

    for t in range(PAIRS):
        dz = dz_rows[t]
        store(gvh, t, dot(gathered(p_all, 2 * t), dz * low4, TN)
              + dot(gathered(p_all, 2 * t + 1), dz * high4, TN))
    local, away, landing = give_back(gvh, gv_out, 0)

    dz_rest.wait_send()
    g_rest.wait_recv()
    slope = jnp.sum(g_recv[...], axis=0)
    probs = p_own[...]
    mean = jnp.sum(probs * slope, axis=-1, keepdims=True)
    ds_all[chip] = (probs * (slope - mean) * scale).astype(BF16)
    ds_rest = gather(ds_all, 5)
    out_copy.wait()
    g_rest.wait_send()
    local.wait()
    away.wait_send()
    landing.wait_recv()
    ds_rest.wait_send()
    ds_rest.wait_recv()
    ds_side = remote(ds_all, ds_out.at[core], back_send.at[1], back_recv.at[1], sibling)
    ds_side.start()
    ds_local = pltpu.make_async_copy(ds_all, ds_out.at[core], local_sem.at[8])
    ds_local.start()
    ds_local.wait()
    ds_side.wait_send()
    remote(ds_all, ds_out.at[other], back_send.at[1], back_recv.at[1], sibling).wait_recv()


def on_device(planes, row_query, row_key, row_value, column_weight, cotangent):
    own_rows, columns, width = row_query.shape
    share = column_weight.shape[1]
    rows, own_columns, _ = cotangent.shape
    vmem = pltpu.VMEM
    sem = pltpu.SemaphoreType.DMA
    row_shape = jax.ShapeDtypeStruct((own_rows, columns, width), BF16)
    out_shape = jax.ShapeDtypeStruct(cotangent.shape, BF16)
    ds_shape = jax.ShapeDtypeStruct((2, CHIPS, 3, 16, 128), BF16)
    column_output, grad_scores, grad_value = pl.pallas_call(
        functools.partial(kernel, planes),
        out_shape=(out_shape, ds_shape, row_shape),
        in_specs=[pl.BlockSpec(memory_space=pl.ANY)] * 5,
        out_specs=[pl.BlockSpec(memory_space=pl.ANY)] * 3,
        scratch_shapes=[
            vmem((4, 128, HALF), BF16),
            vmem((4, 128, HALF), BF16),
            vmem((4, 128, HALF), BF16),
            vmem((rows, own_columns, width), BF16),
            vmem((2, 128, 768), BF16),
            vmem((2, planes * share, HALF), BF16),
            vmem((128, 256), F32),
            vmem((CHIPS, 3, 16, 128), F32),
            vmem((CHIPS, 3, 16, 128), F32),
            vmem((3, 16, 128), F32),
            vmem((CHIPS, 3, 16, 128), BF16),
            vmem((2 * CHIPS, 16, HALF), BF16),
            vmem((2 * CHIPS, 16, HALF), BF16),
            vmem((256, 768), BF16),
            vmem((18, 256, 128), BF16),
            vmem((18, 256, 128), BF16),
            vmem((2, 128, 768), BF16),
            vmem((rows, own_columns, width), BF16),
            vmem((2 * CHIPS, 16, HALF), BF16),
            vmem((2 * CHIPS, 16, HALF), BF16),
            vmem((PAIRS, 128, 512), BF16),
            vmem((CHIPS, 3, 16, 128), F32),
            vmem((CHIPS, 3, 16, 128), F32),
            vmem((CHIPS, 3, 16, 128), BF16),
            vmem((4, 128, HALF), BF16),
            sem((10,)),
            sem((3,)), sem((3,)),
            sem((2, planes)), sem((2, planes)),
            sem((2, planes)), sem((2, planes)),
            sem((2, planes, 2)), sem((2, planes, 2)),
            sem((6,)), sem((6,)),
            sem((2,)), sem((2,)),
            pltpu.SemaphoreType.REGULAR,
        ],
        compiler_params=pltpu.CompilerParams(
            collective_id=0, has_side_effects=True, vmem_limit_bytes=VMEM_LIMIT
        ),
    )(row_query, row_key, row_value, column_weight.T, cotangent)
    return pl.pallas_call(
        finish,
        out_shape=(out_shape, row_shape, row_shape, row_shape),
        in_specs=[pl.BlockSpec(memory_space=pl.ANY)] * 5,
        out_specs=[pl.BlockSpec(memory_space=pl.ANY)] * 4,
        scratch_shapes=[
            vmem(x.shape, BF16)
            for x in (row_shape, row_shape, ds_shape, out_shape, row_shape, row_shape, row_shape)
        ] + [sem((5,)), sem((6,))],
        compiler_params=pltpu.CompilerParams(vmem_limit_bytes=VMEM_LIMIT),
    )(row_query, row_key, grad_scores, column_output, grad_value)


def solution(mesh):
    planes = mesh.shape["grp"]
    in_specs = (
        P(("grp", "seq"), None, None),
        P(("grp", "seq"), None, None),
        P(("grp", "seq"), None, None),
        P(None, "grp"),
        P("grp", "seq", None),
    )
    out_specs = (
        P("grp", "seq", None),
        P(("grp", "seq"), None, None),
        P(("grp", "seq"), None, None),
        P(("grp", "seq"), None, None),
    )
    return jax.shard_map(
        functools.partial(on_device, planes),
        mesh=mesh, in_specs=in_specs, out_specs=out_specs, check_vma=False,
    )
```

```python
import functools
import math

import jax
import jax.numpy as jnp
from jax import lax
from jax.experimental import pallas as pl
from jax.experimental.pallas import tpu as pltpu
from jax.sharding import PartitionSpec as P

HEADS = 12
HEAD_DIM = 64
CHIPS = 16
SIDE = 4
HALF = 384
PAIRS = 3
MESH = pl.DeviceIdType.MESH
VMEM_LIMIT = 60 * 1024 * 1024
F32 = jnp.float32
BF16 = jnp.bfloat16

NN = (((1,), (0,)), ((), ()))
NT = (((1,), (1,)), ((), ()))
TN = (((0,), (0,)), ((), ()))


def dot(x, y, dims):
    return lax.dot_general(x, y, dims, preferred_element_type=F32)


def finish(
    q_in, k_in, ds_in, out_in, gv_in,
    out, gq_out, gk_out, gv_out,
    q, k, ds, out_held, gv_held, gq, gk, in_sem, out_sem,
):
    low, high = head_masks(2)
    arrive = [
        pltpu.make_async_copy(src, dst, in_sem.at[n])
        for n, (src, dst) in enumerate(
            ((ds_in, ds), (k_in, k), (q_in, q), (out_in, out_held), (gv_in, gv_held))
        )
    ]
    for copy in arrive:
        copy.start()
    leave = [
        pltpu.make_async_copy(out_held, out, out_sem.at[0]),
        pltpu.make_async_copy(gv_held, gv_out, out_sem.at[1]),
    ]

    def gradient(held, other, dims, target, n):
        for t in range(2 * PAIRS):
            lanes = slice(128 * t, 128 * t + 128)
            x = jnp.concatenate([other[r, :, lanes] for r in range(2)], axis=1)
            total = None
            for e, keep in enumerate((low, high)):
                h = 2 * t + e
                group, place = h % 6 // 3, h % 3
                rows = jnp.concatenate(
                    [ds[h // 6, 8 * group + b, place] for b in range(8)], axis=0
                )
                part = dot(rows, x * keep, dims)
                total = part if total is None else total + part
            for r in range(2):
                held[r, :, lanes] = total[:, 128 * r : 128 * r + 128].astype(BF16)
            if t % PAIRS == PAIRS - 1:
                half = pl.ds(t // PAIRS * HALF, HALF)
                leave.append(
                    pltpu.make_async_copy(
                        held.at[:, :, half], target.at[:, :, half], out_sem.at[n + t // PAIRS]
                    )
                )
                leave[-1].start()

    arrive[0].wait()
    arrive[1].wait()
    gradient(gq, k, NN, gq_out, 2)
    for n in range(2):
        arrive[3 + n].wait()
        leave[n].start()
    arrive[2].wait()
    gradient(gk, q, TN, gk_out, 4)
    for copy in leave:
        copy.wait()


def head_masks(copies):
    lane = lax.broadcasted_iota(jnp.int32, (1, 128), 1)
    low = jnp.where(lane < HEAD_DIM, 1.0, 0.0).astype(BF16)
    high = jnp.where(lane < HEAD_DIM, 0.0, 1.0).astype(BF16)
    return [jnp.concatenate([x] * copies, axis=1) for x in (low, high)]


def kernel(
    planes,
    q_in, k_in, v_in, w_in, cot_in,
    out, ds_out, gv_out,
    qh, kh, vh, cot4, cot, weight, bias,
    s_send, s_recv, p_own, p_all, z_send, z_recv, zh, abe, dabe, outh, out4,
    dz_send, dz_recv, dz_rows, g_send, g_recv, ds_all, gvh,
    local_sem, swap_send, swap_recv, ring_send, ring_recv, mate_send, mate_recv,
    side_send, side_recv,
    many_send, many_recv, back_send, back_recv, row_sem,
):
    grp = lax.axis_index("grp")
    me = lax.axis_index("seq")
    chip = lax.div(me, 2)
    core = lax.rem(me, 2)
    other = 1 - core
    chip_x, chip_y = lax.rem(chip, SIDE), lax.div(chip, SIDE)
    sibling = (grp, chip * 2 + other)
    far = planes // 2
    reach = (far, planes - 1 - far)

    def plane(step):
        return lax.rem(grp + planes + step, planes)

    scale = 1.0 / (math.sqrt(HEAD_DIM) * math.sqrt(4 * CHIPS))

    def hops(k):
        return min(k % SIDE, SIDE - k % SIDE) + min(k // SIDE, SIDE - k // SIDE)

    targets = [
        lax.rem(chip_y + k // SIDE, SIDE) * SIDE + lax.rem(chip_x + k % SIDE, SIDE)
        for k in sorted(range(1, CHIPS), key=lambda k: -hops(k))
    ]

    def remote(src, dst, send, recv, device):
        return pltpu.make_async_remote_copy(
            src_ref=src, dst_ref=dst, send_sem=send, recv_sem=recv,
            device_id=device, device_id_type=MESH,
        )

    barrier = pltpu.get_barrier_semaphore()
    near = (-2, 2, -1, 1)
    column = [(grp, (lax.rem(chip_y + n, SIDE) * SIDE + chip_x) * 2 + core) for n in (2, 1, 3)]
    row = [(grp, (chip_y * SIDE + lax.rem(chip_x + n, SIDE)) * 2 + core) for n in (2, 1, 3)]
    greeted = row + column + [(plane(step), me) for step in near] + [sibling]
    for device in greeted:
        pl.semaphore_signal(barrier, inc=1, device_id=device, device_id_type=MESH)

    mine = pl.ds(pl.multiple_of(core * HALF, HALF), HALF)
    theirs = pl.ds(pl.multiple_of(other * HALF, HALF), HALF)
    own_rows = pl.ds(core * 2, 2)
    their_rows = pl.ds(other * 2, 2)
    swaps, locals_ = [], []
    for n, (src, dst) in enumerate(((q_in, qh), (k_in, kh), (v_in, vh))):
        swaps.append(
            remote(src.at[:, :, theirs], dst.at[own_rows], swap_send.at[n], swap_recv.at[n], sibling)
        )
        locals_.append(
            pltpu.make_async_copy(src.at[:, :, mine], dst.at[own_rows], local_sem.at[n])
        )
    for n in range(3):
        locals_[n].start()

    share = w_in.shape[0]
    lead = (share // 16 + 1) // 2 * 16
    tail = share - lead
    parity = (lax.rem(chip_x, 2), lax.rem(chip_y, 2))
    mate = (
        (grp, (chip + 1 - 2 * parity[0]) * 2 + core),
        (grp, (chip + SIDE - 2 * SIDE * parity[1]) * 2 + core),
    )

    def block_begin(way, distance):
        return plane(distance if way else -distance) * share

    def part_rows(way, distance, part):
        begin = (parity[way] * tail, parity[way] * lead, (1 - parity[way]) * lead)[part]
        size = (lead, tail, tail)[part]
        return pl.ds(pl.multiple_of(block_begin(way, distance) + begin, 16), size)

    def ring_copy(way, distance):
        jump = 2 - distance % 2
        begin = distance - jump
        rows = part_rows(way, begin, 0)
        if begin == 0:
            src = w_in.at[pl.ds(pl.multiple_of(parity[way] * tail, 16), lead), mine]
        else:
            src = weight.at[core, rows]
        return remote(
            src, weight.at[core, rows], ring_send.at[way, distance],
            ring_recv.at[way, distance], (plane(-jump if way else jump), me),
        )

    def mate_copy(way, distance):
        rows = weight.at[core, part_rows(way, distance, 1)]
        return remote(rows, rows, mate_send.at[way, distance], mate_recv.at[way, distance], mate[way])

    def mate_landing(way, distance):
        rows = weight.at[core, part_rows(way, distance, 2)]
        return remote(rows, rows, mate_send.at[way, distance], mate_recv.at[way, distance], mate[way])

    def side_copy(way, distance, part):
        rows = weight.at[core, part_rows(way, distance, 2 * part)]
        return remote(
            rows, rows, side_send.at[way, distance, part], side_recv.at[way, distance, part], sibling
        )

    def side_landing(way, distance, part):
        rows = weight.at[other, part_rows(way, distance, 2 * part)]
        return remote(
            rows, rows, side_send.at[way, distance, part], side_recv.at[way, distance, part], sibling
        )

    def ring_start(begin):
        for way in range(2):
            for distance in (begin + 2, begin + 1):
                if distance <= reach[way]:
                    ring_copy(way, distance).start()

    def ring_arrive(distance):
        for way in range(2):
            if distance <= reach[way]:
                ring_copy(way, distance).wait_recv()

    def share_start(distance):
        for way in range(2):
            if distance <= reach[way]:
                mate_copy(way, distance).start()
                side_copy(way, distance, 0).start()

    def ring(begin):
        ring_arrive(begin)
        ring_start(begin)
        share_start(begin)
        ring_arrive(begin - 1)
        share_start(begin - 1)

    def mated(begin):
        for distance in (begin, begin - 1):
            for way in range(2):
                if distance <= reach[way]:
                    mate_landing(way, distance).wait_recv()
                    side_copy(way, distance, 1).start()

    weight_own = [
        pltpu.make_async_copy(
            w_in.at[:, pl.ds(half * HALF, HALF)],
            weight.at[half, pl.ds(pl.multiple_of(block_begin(0, 0), 16), share)], local_sem.at[3 + half],
        )
        for half in range(2)
    ]
    for copy in weight_own:
        copy.start()
    cot_copy = pltpu.make_async_copy(cot_in, cot4, local_sem.at[5])
    cot_copy.start()

    pl.semaphore_wait(barrier, len(greeted))
    for device in column:
        pl.semaphore_signal(row_sem, inc=1, device_id=device, device_id_type=MESH)
    ring_start(0)

    for n in range(2):
        swaps[n].start()

    low, high = head_masks(1)
    low4, high4 = head_masks(4)
    row_id = lax.broadcasted_iota(jnp.int32, (128, 256), 0)
    col_id = lax.broadcasted_iota(jnp.int32, (128, 256), 1)
    bias[...] = jnp.where(lax.rem(row_id, 2) == lax.rem(col_id, 2), 0.0, -1e30)

    def wide(ref, t):
        return jnp.concatenate([ref[r, :, 128 * t : 128 * t + 128] for r in range(4)], axis=1)

    def terms(left, right, send_ref, t):
        for e, keep in enumerate((low4, high4)):
            h = 2 * t + e
            part = dot(left, right * keep, NT)
            send_ref[8 * (h // 3) : 8 * (h // 3) + 8, h % 3] = part.reshape(8, 16, 128)

    def gathered(ref, h):
        return ref[8 * (h // 3) : 8 * (h // 3) + 8, h % 3].reshape(128, 128)

    def scatter(send_ref, recv_ref, n):
        for to in targets:
            remote(
                send_ref.at[to], recv_ref.at[chip], many_send.at[n], many_recv.at[n],
                (grp, to * 2 + core),
            ).start()
        recv_ref[chip] = send_ref[chip]
        rest = pl.ds(0, CHIPS - 1)
        return remote(
            send_ref.at[rest], recv_ref.at[rest], many_send.at[n], many_recv.at[n], sibling
        )

    def gather(ref, n):
        for to in targets:
            remote(
                ref.at[chip], ref.at[chip], many_send.at[n], many_recv.at[n],
                (grp, to * 2 + core),
            ).start()
        rest = pl.ds(0, CHIPS - 1)
        return remote(ref.at[rest], ref.at[rest], many_send.at[n], many_recv.at[n], sibling)

    def send_block(send_ref, recv_ref, n, to):
        remote(
            send_ref.at[to], recv_ref.at[me], many_send.at[n], many_recv.at[n], (grp, to)
        ).start()

    def exchange_end(send_ref, recv_ref, n):
        send_block(send_ref, recv_ref, n, chip * 2 + other)
        recv_ref[me] = send_ref[me]
        rest = pl.ds(0, 2 * CHIPS - 1)
        return remote(
            send_ref.at[rest], recv_ref.at[rest], many_send.at[n], many_recv.at[n], sibling
        )

    sublane = lax.broadcasted_iota(jnp.int32, (16, 8, 128), 1)
    first4 = sublane < 4
    first2 = lax.rem(sublane, 4) < 2

    def swap4(x, y):
        return jnp.where(first4, x, pltpu.roll(y, 4, 1)), jnp.where(first4, pltpu.roll(x, 4, 1), y)

    def swap2(x, y):
        return jnp.where(first2, x, pltpu.roll(y, 2, 1)), jnp.where(first2, pltpu.roll(x, 6, 1), y)

    for n in range(2):
        swaps[n].wait_recv()
        locals_[n].wait()
    for t in range(PAIRS):
        terms(wide(qh, t), wide(kh, t), s_send, t)
    pl.semaphore_wait(row_sem, len(column))
    s_all = scatter(s_send, s_recv, 0)
    swaps[2].start()
    ring(2)
    s_all.wait_recv()
    scores = jnp.sum(s_recv[...], axis=0) * scale
    shifted = jnp.exp(scores - jnp.max(scores, axis=-1, keepdims=True))
    probs = shifted / jnp.sum(shifted, axis=-1, keepdims=True)
    p_own[...] = probs
    p_all[chip] = probs.astype(BF16)
    p_rest = gather(p_all, 1)
    cot_copy.wait()
    for u in range(6):
        lanes = slice(128 * u, 128 * u + 128)
        g4 = cot4[:, :, lanes].astype(F32)
        for c in range(2):
            cot[c, :, lanes] = g4[:, 2 * c : 2 * c + 2].reshape(128, 128).astype(BF16)
    ring(4)
    mated(2)
    swaps[2].wait_recv()
    locals_[2].wait()
    p_rest.wait_recv()

    for t in range(PAIRS):
        values = wide(vh, t)
        z = dot(gathered(p_all, 2 * t), values * low4, NN) + dot(
            gathered(p_all, 2 * t + 1), values * high4, NN
        )
        rows = [z[:, 128 * r : 128 * r + 128].reshape(16, 8, 128) for r in range(4)]
        lanes = slice(128 * t, 128 * t + 128)
        for c, (x, y) in enumerate(zip(swap4(rows[0], rows[2]), swap4(rows[1], rows[3]))):
            block = jnp.concatenate(swap2(x, y), axis=1).astype(BF16)
            for n in range(CHIPS):
                z_send[2 * n + c, :, lanes] = block[n]
    for to in targets:
        send_block(z_send, z_recv, 2, to * 2 + core)
        send_block(z_send, z_recv, 2, to * 2 + other)
    z_rest = exchange_end(z_send, z_recv, 2)
    for begin in range(6, far + 1, 2):
        ring(begin)
        mated(begin - 2)
    mated(far)

    for copy in weight_own:
        copy.wait()
    for way in range(2):
        for distance in range(1, reach[way] + 1):
            for part in range(2):
                side_landing(way, distance, part).wait_recv()
    z_rest.wait_recv()

    arrived = z_recv[...].reshape(CHIPS, 2, 16, HALF)
    for half in range(2):
        for t in range(PAIRS):
            z = arrived[:, half, :, 128 * t : 128 * t + 128].astype(F32)
            lanes = slice(half * HALF + 128 * t, half * HALF + 128 * t + 128)
            for c in range(2):
                zh[128 * c : 128 * c + 128, lanes] = (
                    z[:, 8 * c : 8 * c + 8].reshape(128, 128).astype(BF16)
                )
    for part in range(3):
        rows = slice(part * 768, part * 768 + 768)
        w = jnp.concatenate([weight[0, rows], weight[1, rows]], axis=1)
        packed = dot(zh[...], w, NT).astype(BF16)
        for u in range(6):
            abe[6 * part + u] = packed[:, 128 * u : 128 * u + 128]

    @pl.loop(0, 6, unroll=6)
    def _(u):
        lanes = pl.ds(pl.multiple_of(u * 128, 128), 128)
        both = range(2)
        rows = [slice(128 * c, 128 * c + 128) for c in both]
        split = lambda x: jnp.concatenate([x * low, x * high], axis=0)
        stack = lambda x: jnp.concatenate([x[:, :128], x[:, 128:]], axis=0)
        a, b, e = ([abe[6 * n + u, rows[c]] for c in both] for n in range(3))
        g = [cot[c, :, lanes] for c in both]
        a2, b2, e2, g2 = ([split(x) for x in xs] for xs in (a, b, e, g))
        logits = [dot(b[c], a2[c], NT) * 0.125 + bias[...] for c in both]
        slope = [dot(e[c], g2[c], NT) for c in both]
        shifted = [jnp.exp(x - jnp.max(x, axis=0, keepdims=True)) for x in logits]
        weights = [x * (1.0 / jnp.sum(x, axis=0, keepdims=True)) for x in shifted]
        weights_low = [x.astype(BF16) for x in weights]
        mean = [jnp.sum(x * y, axis=0, keepdims=True) for x, y in zip(weights, slope)]
        dlogits = [
            (weights[c] * (slope[c] - mean[c]) * 0.125).astype(BF16) for c in both
        ]
        for c in both:
            att = zh[rows[c], lanes].astype(F32) + dot(stack(weights_low[c]), e2[c], TN)
            outh[c, :, lanes] = att.astype(BF16)
            dabe[12 + u, rows[c]] = dot(weights_low[c], g2[c], NN).astype(BF16)
            dabe[u, rows[c]] = dot(stack(dlogits[c]), b2[c], TN).astype(BF16)
            dabe[6 + u, rows[c]] = dot(dlogits[c], a2[c], NN).astype(BF16)

    dpacked = jnp.concatenate([dabe[n] for n in range(18)], axis=1)
    pieces = [
        dot(dpacked, weight[0, :, :256], NN),
        dot(dpacked, jnp.concatenate([weight[0, :, 256:], weight[1, :, :128]], axis=1), NN),
    ]
    for half in range(2):
        lanes = slice(half * HALF, half * HALF + HALF)
        if half == 0:
            back = jnp.concatenate([pieces[0], pieces[1][:, :128]], axis=1)
        else:
            last = dot(dpacked, weight[1, :, 128:], NN)
            back = jnp.concatenate([pieces[1][:, 128:], last], axis=1)
        blocks = jnp.concatenate(
            [
                (cot[c, :, lanes].astype(F32) + back[128 * c : 128 * c + 128]).reshape(16, 8, HALF)
                for c in range(2)
            ],
            axis=1,
        ).astype(BF16)
        for n in range(CHIPS):
            dz_send[2 * n + half] = blocks[n]
        for to in targets:
            send_block(dz_send, dz_recv, 3, to * 2 + half)
    dz_rest = exchange_end(dz_send, dz_recv, 3)

    for u in range(6):
        lanes = slice(128 * u, 128 * u + 128)
        out4[:, :, lanes] = jnp.concatenate(
            [outh[c, :, lanes].astype(F32).reshape(64, 2, 128) for c in range(2)], axis=1
        ).astype(BF16)
    out_copy = pltpu.make_async_copy(out4, out, local_sem.at[6])
    out_copy.start()
    for copy in swaps:
        copy.wait_send()
    for way in range(2):
        for distance in range(1, reach[way] + 1):
            ring_copy(way, distance).wait_send()
            mate_copy(way, distance).wait_send()
            for part in range(2):
                side_copy(way, distance, part).wait_send()
    for rest in (s_all, p_rest, z_rest):
        rest.wait_send()
    dz_rest.wait_recv()

    for t in range(PAIRS):
        lanes = slice(128 * t, 128 * t + 128)
        blocks = dz_recv[...].reshape(CHIPS, 2, 16, HALF)[:, :, :, lanes].astype(F32)
        x02, x13 = zip(*[swap2(blocks[:, c, :8], blocks[:, c, 8:]) for c in range(2)])
        r0, r2 = swap4(*x02)
        r1, r3 = swap4(*x13)
        dz = jnp.concatenate(
            [x.reshape(128, 128).astype(BF16) for x in (r0, r1, r2, r3)], axis=1
        )
        dz_rows[t] = dz
        terms(dz, wide(vh, t), g_send, t)
    g_rest = scatter(g_send, g_recv, 4)

    def store(ref, t, x):
        for r in range(4):
            ref[r, :, 128 * t : 128 * t + 128] = x[:, 128 * r : 128 * r + 128].astype(BF16)

    def give_back(ref, out_ref, n):
        local = pltpu.make_async_copy(ref.at[own_rows], out_ref.at[:, :, mine], local_sem.at[7 + n])
        away = remote(
            ref.at[their_rows], out_ref.at[:, :, mine], back_send.at[n], back_recv.at[n], sibling
        )
        landing = remote(
            ref.at[their_rows], out_ref.at[:, :, theirs], back_send.at[n], back_recv.at[n], sibling
        )
        local.start()
        away.start()
        return local, away, landing

    for t in range(PAIRS):
        dz = dz_rows[t]
        store(gvh, t, dot(gathered(p_all, 2 * t), dz * low4, TN)
              + dot(gathered(p_all, 2 * t + 1), dz * high4, TN))
    local, away, landing = give_back(gvh, gv_out, 0)

    dz_rest.wait_send()
    g_rest.wait_recv()
    slope = jnp.sum(g_recv[...], axis=0)
    probs = p_own[...]
    mean = jnp.sum(probs * slope, axis=-1, keepdims=True)
    ds_all[chip] = (probs * (slope - mean) * scale).astype(BF16)
    ds_rest = gather(ds_all, 5)
    out_copy.wait()
    g_rest.wait_send()
    local.wait()
    away.wait_send()
    landing.wait_recv()
    ds_rest.wait_send()
    ds_rest.wait_recv()
    ds_side = remote(ds_all, ds_out.at[core], back_send.at[1], back_recv.at[1], sibling)
    ds_side.start()
    ds_local = pltpu.make_async_copy(ds_all, ds_out.at[core], local_sem.at[8])
    ds_local.start()
    ds_local.wait()
    ds_side.wait_send()
    remote(ds_all, ds_out.at[other], back_send.at[1], back_recv.at[1], sibling).wait_recv()


def on_device(planes, row_query, row_key, row_value, column_weight, cotangent):
    own_rows, columns, width = row_query.shape
    share = column_weight.shape[1]
    rows, own_columns, _ = cotangent.shape
    vmem = pltpu.VMEM
    sem = pltpu.SemaphoreType.DMA
    row_shape = jax.ShapeDtypeStruct((own_rows, columns, width), BF16)
    out_shape = jax.ShapeDtypeStruct(cotangent.shape, BF16)
    ds_shape = jax.ShapeDtypeStruct((2, CHIPS, 3, 16, 128), BF16)
    column_output, grad_scores, grad_value = pl.pallas_call(
        functools.partial(kernel, planes),
        out_shape=(out_shape, ds_shape, row_shape),
        in_specs=[pl.BlockSpec(memory_space=pl.ANY)] * 5,
        out_specs=[pl.BlockSpec(memory_space=pl.ANY)] * 3,
        scratch_shapes=[
            vmem((4, 128, HALF), BF16),
            vmem((4, 128, HALF), BF16),
            vmem((4, 128, HALF), BF16),
            vmem((rows, own_columns, width), BF16),
            vmem((2, 128, 768), BF16),
            vmem((2, planes * share, HALF), BF16),
            vmem((128, 256), F32),
            vmem((CHIPS, 3, 16, 128), F32),
            vmem((CHIPS, 3, 16, 128), F32),
            vmem((3, 16, 128), F32),
            vmem((CHIPS, 3, 16, 128), BF16),
            vmem((2 * CHIPS, 16, HALF), BF16),
            vmem((2 * CHIPS, 16, HALF), BF16),
            vmem((256, 768), BF16),
            vmem((18, 256, 128), BF16),
            vmem((18, 256, 128), BF16),
            vmem((2, 128, 768), BF16),
            vmem((rows, own_columns, width), BF16),
            vmem((2 * CHIPS, 16, HALF), BF16),
            vmem((2 * CHIPS, 16, HALF), BF16),
            vmem((PAIRS, 128, 512), BF16),
            vmem((CHIPS, 3, 16, 128), F32),
            vmem((CHIPS, 3, 16, 128), F32),
            vmem((CHIPS, 3, 16, 128), BF16),
            vmem((4, 128, HALF), BF16),
            sem((10,)),
            sem((3,)), sem((3,)),
            sem((2, planes)), sem((2, planes)),
            sem((2, planes)), sem((2, planes)),
            sem((2, planes, 2)), sem((2, planes, 2)),
            sem((6,)), sem((6,)),
            sem((2,)), sem((2,)),
            pltpu.SemaphoreType.REGULAR,
        ],
        compiler_params=pltpu.CompilerParams(
            collective_id=0, has_side_effects=True, vmem_limit_bytes=VMEM_LIMIT
        ),
    )(row_query, row_key, row_value, column_weight.T, cotangent)
    return pl.pallas_call(
        finish,
        out_shape=(out_shape, row_shape, row_shape, row_shape),
        in_specs=[pl.BlockSpec(memory_space=pl.ANY)] * 5,
        out_specs=[pl.BlockSpec(memory_space=pl.ANY)] * 4,
        scratch_shapes=[
            vmem(x.shape, BF16)
            for x in (row_shape, row_shape, ds_shape, out_shape, row_shape, row_shape, row_shape)
        ] + [sem((5,)), sem((6,))],
        compiler_params=pltpu.CompilerParams(vmem_limit_bytes=VMEM_LIMIT),
    )(row_query, row_key, grad_scores, column_output, grad_value)


def solution(mesh):
    planes = mesh.shape["grp"]
    in_specs = (
        P(("grp", "seq"), None, None),
        P(("grp", "seq"), None, None),
        P(("grp", "seq"), None, None),
        P(None, "grp"),
        P("grp", "seq", None),
    )
    out_specs = (
        P("grp", "seq", None),
        P(("grp", "seq"), None, None),
        P(("grp", "seq"), None, None),
        P(("grp", "seq"), None, None),
    )
    return jax.shard_map(
        functools.partial(on_device, planes),
        mesh=mesh, in_specs=in_specs, out_specs=out_specs, check_vma=False,
    )
```
